512 devices in a mesh: fsdp: 16 (over z, core), tp: 32 (over y, x).
Axes of the slice: x: 4, y: 8, z: 8, core: 2. Of those that a mesh axis runs over, the one named last changes fastest.
Arguments:
- momentum: bfloat16 [8192, 14336], P('fsdp', 'tp'), may hold values from -6 to 6
- grad: bfloat16 [8192, 14336], P('fsdp', 'tp'), may hold values from -80 to 80
- basis: bfloat16 [14336, 1024], P('tp', 'fsdp'), may hold values from -6 to 6
Outputs:
- momentum_new: bfloat16 [8192, 14336], P('fsdp', 'tp')
- basis_new: bfloat16 [14336, 1024], P('tp', 'fsdp')
- update: bfloat16 [8192, 14336], P('fsdp', 'tp')
The draws below stay inside these ranges and needn't reach their ends.
All inputs are finite; a program needn't handle non-finite values.
Results may differ from the reference program's by a relative error of at most 0.018.
Values may be sent and summed in bfloat16 or wider, within the bound.
No kernel may reach another device: no remote copies, remote signals or barrier semaphores. Data moves between devices by JAX's collectives and lax.ppermute only.
A program may use at most 64 MiB of HBM per device.

```python
import math
import jax
import jax.numpy as jnp
from jax import lax

M = 8192
N = 14336
R = 1024


def draw_grad(key, part):
    key = jax.random.fold_in(key, 11)
    base_key, col_key = jax.random.split(key, 2)
    position = jnp.arange(N, dtype=jnp.float32) / N
    col_scale = jnp.exp(jnp.log(3.0) * position) * jnp.exp(jax.random.uniform(col_key, (N,), jnp.float32, 0.0, jnp.log(10.0)))
    values = jnp.clip(jax.random.normal(base_key, (M, N), jnp.float32), -4.0, 4.0)
    return (0.15 * values * col_scale[None, :]).astype(jnp.bfloat16)


def block_scale(stream_key, shape, cuts, smallest, largest):
    loudness, own = 1.0, jax.random.fold_in(stream_key, 6)
    for dim, parts in cuts:
        heights = jnp.exp(jax.random.uniform(jax.random.fold_in(own, dim), (parts,), jnp.float32, smallest / len(cuts), largest / len(cuts)))
        loudness = loudness * jnp.repeat(heights, shape[dim] // parts).reshape([-1 if axis == dim else 1 for axis in range(len(shape))])
    return loudness


def gaussian(rng, dims, deviation, limit, cuts=(), kind=jnp.bfloat16):
    factor_of = block_scale(rng, dims, cuts, -0.22, 0.18) if cuts else 1.0
    entries = jax.random.normal(rng, dims, jnp.float32) * deviation * factor_of
    return jnp.minimum(jnp.maximum(entries, -limit), limit).astype(kind)


def setup_inputs(seed: int = 0) -> dict:
    arg_keys = jax.random.split(jax.random.key(seed), 4)
    return {
        "momentum": gaussian(arg_keys[0], (M, N), 1.0, 6.0, ((0, 16), (1, 32))),
        "grad": draw_grad(jax.random.fold_in(arg_keys[3], 71), 0),
        "basis": gaussian(arg_keys[2], (N, R), 1.0, 6.0, ((0, 32), (1, 16))),
    }


keep_rate = 0.95
epsilon = 1e-06

def reference(momentum, grad, basis):
    total = momentum.astype(jnp.float32) + grad.astype(jnp.float32)
    total_b = total.astype(jnp.bfloat16)
    left = jnp.dot(total_b.astype(jnp.float32), basis.astype(jnp.float32), preferred_element_type=jnp.float32)
    gram = jnp.dot(left.T, left, precision=lax.Precision.HIGHEST)
    chol = jnp.linalg.cholesky(gram)
    ortho = lax.linalg.triangular_solve(chol, left, left_side=False, lower=True, transpose_a=True)
    ortho_b = ortho.astype(jnp.bfloat16)
    right = lax.dot_general(total_b.astype(jnp.float32), ortho_b.astype(jnp.float32), (((0,), (0,)), ((), ())), preferred_element_type=jnp.float32)
    scale = jnp.sqrt(lax.optimization_barrier(jnp.sum(right * right, axis=0)) / N + epsilon)
    basis_b = (right / scale[None, :]).astype(jnp.bfloat16)
    right_b = right.astype(jnp.bfloat16)
    correction = lax.dot_general(ortho_b.astype(jnp.float32), right_b.astype(jnp.float32), (((1,), (1,)), ((), ())), preferred_element_type=jnp.float32)
    momentum_new = (total - (1.0 - keep_rate) * correction).astype(jnp.bfloat16)
    raw = lax.dot_general(ortho_b.astype(jnp.float32), basis_b.astype(jnp.float32), (((1,), (1,)), ((), ())), preferred_element_type=jnp.float32)
    update = (math.sqrt(M / R) * raw).astype(jnp.bfloat16)
    return (momentum_new, basis_b, update)
```

```python
import math

import jax
import jax.numpy as jnp
from jax import lax
from jax.sharding import PartitionSpec as P

keep_rate = 0.95
epsilon = 1e-06


def groups(n_fsdp):
    z_groups = [[2 * z + c for z in range(n_fsdp // 2)] for c in range(2)]
    core_groups = [[2 * z, 2 * z + 1] for z in range(n_fsdp // 2)]
    return z_groups, core_groups


def exchange(pieces, axis, index_groups=None):
    return lax.all_to_all(pieces, axis, 0, 0, tiled=True, axis_index_groups=index_groups)


def collect(own, axis, count, index_groups=None):
    copies = jnp.broadcast_to(own[None], (count,) + own.shape)
    return exchange(copies, axis, index_groups)


def split_parts(value):
    high = value.astype(jnp.bfloat16)
    low = (value - high.astype(jnp.float32)).astype(jnp.bfloat16)
    return high, low


def per_device(momentum, grad, basis):
    n_fsdp, n_tp = lax.axis_size("fsdp"), lax.axis_size("tp")
    n_z = n_fsdp // 2
    z_groups, core_groups = groups(n_fsdp)
    rows, cols = momentum.shape
    share = basis.shape[1]
    rank = share * n_fsdp
    rows_all, cols_all = rows * n_fsdp, cols * n_tp
    me_fsdp, me_tp = lax.axis_index("fsdp"), lax.axis_index("tp")

    total = momentum.astype(jnp.float32) + grad.astype(jnp.float32)
    total_b = total.astype(jnp.bfloat16)
    basis_all = lax.all_gather(basis, "fsdp", axis=1, tiled=True)
    part = jnp.dot(total_b, basis_all, preferred_element_type=jnp.float32)
    left_own = jnp.sum(exchange(part.reshape(n_tp, rows // n_tp, rank), "tp"), axis=0)
    left = collect(left_own, "tp", n_tp).reshape(rows, rank)

    slab = rank // n_tp
    mine = lax.dynamic_slice_in_dim(left, me_tp * slab, slab, 1)
    gram_part = lax.dot_general(
        mine, left, (((0,), (0,)), ((), ())), precision=lax.Precision.HIGHEST
    )
    half = jnp.sum(
        exchange(gram_part.reshape(2, slab // 2, rank), "fsdp", core_groups), axis=0
    )
    half = jnp.sum(collect(half, "fsdp", n_z, z_groups), axis=0)
    own_half = collect(half, "tp", n_tp)
    other_half = lax.ppermute(own_half, "fsdp", [(i, i ^ 1) for i in range(n_fsdp)])
    first = (me_fsdp % 2) == 0
    gram = jnp.stack(
        [jnp.where(first, own_half, other_half), jnp.where(first, other_half, own_half)], axis=1
    ).reshape(rank, rank)

    high, low = split_parts(left)
    dims = (((0,), (0,)), ((), ()))
    back = lax.dot_general(total_b, high, dims, preferred_element_type=jnp.float32)
    back = back + lax.dot_general(total_b, low, dims, preferred_element_type=jnp.float32)
    padded = -(-cols // (8 * n_fsdp)) * 8 * n_fsdp
    back = jnp.pad(back, ((0, padded - cols), (0, 0)))
    back = lax.psum_scatter(back, "fsdp", scatter_dimension=0, tiled=True)
    back = lax.all_gather(back, "fsdp", axis=0, tiled=True)[:cols]

    chol = jnp.linalg.cholesky(gram)
    solved = lax.linalg.triangular_solve(
        chol, jnp.concatenate([left, back]), left_side=False, lower=True, transpose_a=True
    )
    ortho_b = solved[:rows].astype(jnp.bfloat16)
    right = solved[rows:]
    squares = collect(jnp.sum(right * right, axis=0)[None], "tp", n_tp)
    scale = jnp.sqrt(jnp.sum(squares, axis=(0, 1)) / cols_all + epsilon)
    right_b = right.astype(jnp.bfloat16)
    basis_full = (right / scale[None, :]).astype(jnp.bfloat16)
    basis_new = lax.dynamic_slice_in_dim(basis_full, me_fsdp * share, share, 1)
    correction = lax.dot_general(
        ortho_b, right_b, (((1,), (1,)), ((), ())), preferred_element_type=jnp.float32
    )
    raw = lax.dot_general(
        ortho_b, basis_full, (((1,), (1,)), ((), ())), preferred_element_type=jnp.float32
    )
    momentum_new = (total - (1.0 - keep_rate) * correction).astype(jnp.bfloat16)
    update = (math.sqrt(rows_all / rank) * raw).astype(jnp.bfloat16)
    return (momentum_new, basis_new, update)


def solution(mesh):
    return jax.shard_map(
        per_device,
        mesh=mesh,
        in_specs=(P("fsdp", "tp"), P("fsdp", "tp"), P("tp", "fsdp")),
        out_specs=(P("fsdp", "tp"), P("tp", "fsdp"), P("fsdp", "tp")),
        check_vma=False,
    )
```

```python
import functools
import math

import jax
import jax.numpy as jnp
from jax import lax
from jax.experimental import pallas as pl
from jax.experimental.pallas import tpu as pltpu
from jax.sharding import PartitionSpec as P

keep_rate = 0.95
epsilon = 1e-06
BLOCK = 128
SUB = 8
HI = lax.Precision.HIGHEST


def groups(n_fsdp):
    z_groups = [[2 * z + c for z in range(n_fsdp // 2)] for c in range(2)]
    core_groups = [[2 * z, 2 * z + 1] for z in range(n_fsdp // 2)]
    return z_groups, core_groups


def exchange(pieces, axis, index_groups=None):
    return lax.all_to_all(pieces, axis, 0, 0, tiled=True, axis_index_groups=index_groups)


def collect(own, axis, count, index_groups=None):
    copies = jnp.broadcast_to(own[None], (count,) + own.shape)
    return exchange(copies, axis, index_groups)


def split_parts(value):
    high = value.astype(jnp.bfloat16)
    low = (value - high.astype(jnp.float32)).astype(jnp.bfloat16)
    return high, low


def place(t, per_pair, n, strip):
    pair = t // per_pair
    return pair, n - 1 - pair, (t % per_pair) * strip


def add_up(terms):
    while len(terms) > 1:
        terms = [sum(terms[i + 1 : i + 2], terms[i]) for i in range(0, len(terms), 2)]
    return terms[0]


def invert_factor(block, spare):
    n_groups = BLOCK // 8
    lane = lax.broadcasted_iota(jnp.int32, (8, BLOCK), 1)
    sub = lax.broadcasted_iota(jnp.int32, (8, BLOCK), 0)
    rows = [block[8 * g : 8 * g + 8] for g in range(n_groups)]

    def pile(lines):
        result = lines[0]
        for a in range(1, 8):
            result = jnp.where(sub == a, lines[a], result)
        return result

    for begin in range(0, n_groups, SUB):
        end = begin + SUB
        lefts, rights = [], []
        for g in range(begin, end):
            k = 8 * g
            columns = [
                [jnp.broadcast_to(rows[h][:, k + a : k + a + 1], (8, BLOCK)) for h in range(g, end)]
                for a in range(8)
            ]
            inside = (lane >= k) & (lane < k + 8)
            slot = 72 * (g % 2)
            spare[slot : slot + 8, :] = rows[g]
            for a in range(8):
                spare[slot + 8 + 8 * a : slot + 16 + 8 * a, :] = columns[a][0]

            def spread(row):
                return jnp.broadcast_to(spare[slot + row : slot + row + 1, :], (8, BLOCK))

            line = [
                jnp.where(inside, jnp.where(lane == k + a, 1.0, 0.0), spread(a)) for a in range(8)
            ]
            held = {(a, b): spread(8 + 8 * b + a) for a in range(8) for b in range(a, 8)}
            columns = [column[1:] for column in columns]
            scaled, final = [], []
            for a in range(0, 8, 2):
                d = a + 1
                det = held[a, a] * held[d, d] - held[a, d] * held[a, d]
                inverse = 1.0 / held[a, a]
                inverse_d = held[a, a] * (1.0 / det)
                ratio = held[a, d] * inverse
                for c in range(d, 8):
                    held[d, c] = held[d, c] - ratio * held[a, c]
                line[d] = line[d] - ratio * line[a]
                columns[d] = [x - ratio * y for x, y in zip(columns[d], columns[a])]
                for b in range(d + 1, 8):
                    ratio, ratio_d = held[a, b] * inverse, held[d, b] * inverse_d
                    for c in range(b, 8):
                        held[b, c] = held[b, c] - ratio * held[a, c] - ratio_d * held[d, c]
                    line[b] = line[b] - ratio * line[a] - ratio_d * line[d]
                    columns[b] = [
                        x - ratio * y - ratio_d * z
                        for x, y, z in zip(columns[b], columns[a], columns[d])
                    ]
                scaled += [line[a] * inverse, line[d] * inverse_d]
                final += [line[a] * lax.rsqrt(held[a, a]), line[d] * lax.rsqrt(held[d, d])]
            for h in range(g + 1, end):
                taken = add_up([columns[a][h - g - 1] * scaled[a] for a in range(8)])
                rows[h] = jnp.where(inside, 0.0, rows[h]) - taken
            rows[g] = pile(final)
            lefts.append(jnp.where(lane >= 8 * end, rows[g], 0.0))
            rights.append(jnp.where((lane >= k + 8) & (lane < 8 * end), 0.0, rows[g]))
        if end < n_groups:
            taken = dot32(jnp.concatenate(lefts), jnp.concatenate(rights), 0)
            inside = (lane >= 8 * begin) & (lane < 8 * end)
            for h in range(end, n_groups):
                rows[h] = jnp.where(inside, 0.0, rows[h]) - taken[8 * h : 8 * h + 8]
    result = jnp.concatenate(rows, axis=0)
    r = lax.broadcasted_iota(jnp.int32, (BLOCK, BLOCK), 0)
    c = lax.broadcasted_iota(jnp.int32, (BLOCK, BLOCK), 1)
    return jnp.where(c <= r, result, 0.0)


def dot32(a, b, dim=1):
    return lax.dot_general(
        a, b, (((dim,), (0,)), ((), ())), precision=HI, preferred_element_type=jnp.float32
    )


def inverse_kernel(n, n_tp, core_ref, own_ref, other_ref, high_ref, low_ref, work, scale, corner, spare):
    per_pair = n_tp // (n // 2)
    strip = BLOCK // per_pair
    half = strip // 2
    core = core_ref[0]
    for t in range(n_tp):
        first, second, offset = place(t, per_pair, n, strip)
        width = (n - first) * BLOCK
        for source, c in ((own_ref, core), (other_ref, 1 - core)):
            for row, lanes in ((first, slice(0, width)), (second, slice(width, None))):
                start = pl.multiple_of(row * BLOCK + offset + c * half, half)
                work[pl.ds(start, half), row * BLOCK :] = source[t, :, lanes]

    r = lax.broadcasted_iota(jnp.int32, (BLOCK, BLOCK), 0)
    c = lax.broadcasted_iota(jnp.int32, (BLOCK, BLOCK), 1)
    tall = []
    for i in range(n):
        rows = slice(i * BLOCK, (i + 1) * BLOCK)
        diagonal = jnp.where(r == c, work[rows, rows], 0.0)
        scale[:, rows] = lax.rsqrt(jnp.sum(diagonal, axis=0, keepdims=True))
        tall.append(lax.rsqrt(jnp.sum(diagonal, axis=1, keepdims=True)))
    for i in range(n):
        rows, rest = slice(i * BLOCK, (i + 1) * BLOCK), slice(i * BLOCK, None)
        work[rows, rest] = work[rows, rest] * tall[i] * scale[:, rest]

    wide = 2 * BLOCK
    corner[:BLOCK, BLOCK:] = jnp.zeros((BLOCK, BLOCK), jnp.float32)

    @pl.loop(0, n // 2)
    def _(k):
        start = pl.multiple_of(k * wide, wide)
        here, top, bottom = pl.ds(start, wide), pl.ds(start, BLOCK), pl.ds(start + BLOCK, BLOCK)
        one = invert_factor(work[top, top], spare)
        cross = dot32(one, work[top, bottom])
        two = invert_factor(work[bottom, bottom] - dot32(cross, cross, 0), spare)
        corner[:BLOCK, :BLOCK] = one
        corner[BLOCK:, BLOCK:] = two
        corner[BLOCK:, :BLOCK] = -dot32(two, dot32(cross, one, 0))
        work[here, :] = dot32(corner[...], work[here, :])
        work[here, here] = corner[...]

        @pl.loop(k + 1, n // 2)
        def _(i):
            there = pl.ds(pl.multiple_of(i * wide, wide), wide)
            factor = work[here, there]
            work[there, here] = jnp.zeros((wide, wide), jnp.float32)
            work[there, :] -= dot32(factor, work[here, :], 0)

    for i in range(n // 2):
        rows = slice(i * wide, (i + 1) * wide)
        width = (i + 1) * wide
        high, low = split_parts(work[rows, :width] * scale[:, :width])
        high_ref[rows, :width] = high
        low_ref[rows, :width] = low
        if width < n * BLOCK:
            rest = jnp.zeros((wide, n * BLOCK - width), jnp.bfloat16)
            high_ref[rows, width:] = rest
            low_ref[rows, width:] = rest


def inverse_factor(core, own, other, rank):
    n_tp = own.shape[0]
    n = rank // BLOCK
    return pl.pallas_call(
        functools.partial(inverse_kernel, n, n_tp),
        out_shape=[jax.ShapeDtypeStruct((rank, rank), jnp.bfloat16)] * 2,
        in_specs=[pl.BlockSpec(memory_space=pltpu.SMEM)]
        + [pl.BlockSpec(memory_space=pltpu.VMEM)] * 2,
        out_specs=[pl.BlockSpec(memory_space=pltpu.VMEM)] * 2,
        scratch_shapes=[
            pltpu.VMEM((rank, rank), jnp.float32),
            pltpu.VMEM((1, rank), jnp.float32),
            pltpu.VMEM((2 * BLOCK, 2 * BLOCK), jnp.float32),
            pltpu.VMEM((144, BLOCK), jnp.float32),
        ],
        compiler_params=pltpu.CompilerParams(vmem_limit_bytes=40 * 1024 * 1024),
        cost_estimate=pl.CostEstimate(
            flops=12 * rank**3, bytes_accessed=8 * rank**2, transcendentals=0
        ),
    )(core, own, other)


def right_kernel(back_ref, high_ref, low_ref, right_ref, squares_ref):
    high, low = split_parts(back_ref[: right_ref.shape[0], :])
    wide = 2 * BLOCK
    for j in range(high_ref.shape[0] // wide):
        here, depth = slice(j * wide, (j + 1) * wide), slice(0, (j + 1) * wide)
        total = dot16(high[:, depth], high_ref[here, depth])
        total += dot16(high[:, depth], low_ref[here, depth])
        total += dot16(low[:, depth], high_ref[here, depth])
        right_ref[:, here] = total
        squares = jnp.sum(total * total, axis=0, keepdims=True)
        for t in range(squares_ref.shape[0]):
            squares_ref[t, :, here] = squares


def dot16(a, b):
    return lax.dot_general(a, b, (((1,), (1,)), ((), ())), preferred_element_type=jnp.float32)


def project(back, high, low, rows, n_tp):
    rank = back.shape[1]
    return pl.pallas_call(
        right_kernel,
        out_shape=[
            jax.ShapeDtypeStruct((rows, rank), jnp.float32),
            jax.ShapeDtypeStruct((n_tp, 1, rank), jnp.float32),
        ],
        in_specs=[pl.BlockSpec(memory_space=pltpu.VMEM)] * 3,
        out_specs=[pl.BlockSpec(memory_space=pltpu.VMEM)] * 2,
        compiler_params=pltpu.CompilerParams(vmem_limit_bytes=40 * 1024 * 1024),
        cost_estimate=pl.CostEstimate(
            flops=6 * rows * rank**2, bytes_accessed=8 * rank * rows, transcendentals=0
        ),
    )(back, high, low)


def per_device(momentum, grad, basis):
    n_fsdp, n_tp = lax.axis_size("fsdp"), lax.axis_size("tp")
    n_z = n_fsdp // 2
    z_groups, core_groups = groups(n_fsdp)
    rows, cols = momentum.shape
    share = basis.shape[1]
    rank = share * n_fsdp
    rows_all, cols_all = rows * n_fsdp, cols * n_tp
    me_fsdp, me_tp = lax.axis_index("fsdp"), lax.axis_index("tp")
    by_rows = (((0,), (0,)), ((), ()))
    by_cols = (((1,), (1,)), ((), ()))

    def dot(a, b, dims):
        return lax.dot_general(a, b, dims, preferred_element_type=jnp.float32)

    total = momentum.astype(jnp.float32) + grad.astype(jnp.float32)
    total_b = total.astype(jnp.bfloat16)
    basis_all = lax.all_gather(basis, "fsdp", axis=1, tiled=True)
    part = jnp.dot(total_b, basis_all, preferred_element_type=jnp.float32).astype(jnp.bfloat16)
    arrived = exchange(part.reshape(n_tp, rows // n_tp, rank), "tp")
    left_own = jnp.sum(arrived.astype(jnp.float32), axis=0).astype(jnp.bfloat16)
    left = collect(left_own, "tp", n_tp).reshape(rows, rank)

    n = rank // BLOCK
    per_pair = n_tp // (n // 2)
    strip = BLOCK // per_pair
    pair, mirror, offset = place(me_tp, per_pair, n, strip)
    made = []
    for row in (pair, mirror):
        mine = lax.dynamic_slice_in_dim(left, row * BLOCK + offset, strip, 1)
        made.append(dot(mine, left, by_rows))
    packed = lax.select_n(
        pair,
        *[
            jnp.concatenate([made[0][:, p * BLOCK :], made[1][:, (n - 1 - p) * BLOCK :]], axis=1)
            for p in range(n // 2)
        ],
    )
    packed = packed.reshape(2, strip // 2, packed.shape[1])
    packed = jnp.sum(exchange(packed, "fsdp", core_groups), axis=0)
    packed = jnp.sum(collect(packed, "fsdp", n_z, z_groups), axis=0)
    own = collect(packed, "tp", n_tp)
    other = lax.ppermute(own, "fsdp", [(i, i ^ 1) for i in range(n_fsdp)])

    back = dot(total_b, left, by_rows)
    padded = -(-cols // (8 * n_fsdp)) * 8 * n_fsdp
    back = jnp.pad(back, ((0, padded - cols), (0, 0)))
    back = lax.psum_scatter(back, "fsdp", scatter_dimension=0, tiled=True)
    back = lax.all_gather(back, "fsdp", axis=0, tiled=True)

    core = (me_fsdp % 2).astype(jnp.int32).reshape(1)
    inverse_high, inverse_low = inverse_factor(core, own, other, rank)
    right, squares = project(back, inverse_high, inverse_low, cols, n_tp)
    left, squares = lax.optimization_barrier((left, squares))
    squares = exchange(squares, "tp")
    ortho = dot(left, inverse_high, by_cols) + dot(left, inverse_low, by_cols)
    ortho_b = ortho.astype(jnp.bfloat16)
    scale = jnp.sqrt(jnp.sum(squares, axis=(0, 1)) / cols_all + epsilon)
    right_b = right.astype(jnp.bfloat16)
    basis_full = (right / scale[None, :]).astype(jnp.bfloat16)
    basis_new = lax.dynamic_slice_in_dim(basis_full, me_fsdp * share, share, 1)
    correction = dot(ortho_b, right_b, by_cols)
    raw = dot(ortho_b, basis_full, by_cols)
    momentum_new = (total - (1.0 - keep_rate) * correction).astype(jnp.bfloat16)
    update = (math.sqrt(rows_all / rank) * raw).astype(jnp.bfloat16)
    return (momentum_new, basis_new, update)


def solution(mesh):
    return jax.shard_map(
        per_device,
        mesh=mesh,
        in_specs=(P("fsdp", "tp"), P("fsdp", "tp"), P("tp", "fsdp")),
        out_specs=(P("fsdp", "tp"), P("tp", "fsdp"), P("fsdp", "tp")),
        check_vma=False,
    )
```

```python
import functools
import math

import jax
import jax.numpy as jnp
from jax import lax
from jax.experimental import pallas as pl
from jax.experimental.pallas import tpu as pltpu
from jax.sharding import PartitionSpec as P

keep_rate = 0.95
epsilon = 1e-06
BLOCK = 128
SUB = 8
HI = lax.Precision.HIGHEST


def groups(n_fsdp):
    z_groups = [[2 * z + c for z in range(n_fsdp // 2)] for c in range(2)]
    core_groups = [[2 * z, 2 * z + 1] for z in range(n_fsdp // 2)]
    return z_groups, core_groups


def exchange(pieces, axis, index_groups=None):
    return lax.all_to_all(pieces, axis, 0, 0, tiled=True, axis_index_groups=index_groups)


def collect(own, axis, count, index_groups=None):
    copies = jnp.broadcast_to(own[None], (count,) + own.shape)
    return exchange(copies, axis, index_groups)


def split_parts(value):
    high = value.astype(jnp.bfloat16)
    low = (value - high.astype(jnp.float32)).astype(jnp.bfloat16)
    return high, low


def place(t, per_pair, n, strip):
    pair = t // per_pair
    return pair, n - 1 - pair, (t % per_pair) * strip


def add_up(terms):
    while len(terms) > 1:
        terms = [sum(terms[i + 1 : i + 2], terms[i]) for i in range(0, len(terms), 2)]
    return terms[0]


def invert_factor(block, spare, aside):
    n_groups = BLOCK // 8
    lane = lax.broadcasted_iota(jnp.int32, (8, BLOCK), 1)
    sub = lax.broadcasted_iota(jnp.int32, (8, BLOCK), 0)
    rows = [block[8 * g : 8 * g + 8] for g in range(n_groups)]

    def pile(lines):
        result = lines[0]
        for a in range(1, 8):
            result = jnp.where(sub == a, lines[a], result)
        return result

    for begin in range(0, n_groups, SUB):
        end = begin + SUB
        lefts, rights = [], []
        for g in range(begin, end):
            k = 8 * g
            columns = [
                [jnp.broadcast_to(rows[h][:, k + a : k + a + 1], (8, BLOCK)) for h in range(g, end)]
                for a in range(8)
            ]
            inside = (lane >= k) & (lane < k + 8)
            slot = 72 * (g % 2)
            spare[slot : slot + 8, :] = rows[g]
            for a in range(8):
                spare[slot + 8 + 8 * a : slot + 16 + 8 * a, :] = columns[a][0]

            def spread(row):
                return jnp.broadcast_to(spare[slot + row : slot + row + 1, :], (8, BLOCK))

            line = [
                jnp.where(inside, jnp.where(lane == k + a, 1.0, 0.0), spread(a)) for a in range(8)
            ]
            held = {(a, b): spread(8 + 8 * b + a) for a in range(8) for b in range(a, 8)}
            columns = [column[1:] for column in columns]
            scaled, final = [], []
            for a in range(0, 8, 2):
                d = a + 1
                det = held[a, a] * held[d, d] - held[a, d] * held[a, d]
                inverse = 1.0 / held[a, a]
                inverse_d = held[a, a] * (1.0 / det)
                ratio = held[a, d] * inverse
                for c in range(d, 8):
                    held[d, c] = held[d, c] - ratio * held[a, c]
                line[d] = line[d] - ratio * line[a]
                columns[d] = [x - ratio * y for x, y in zip(columns[d], columns[a])]
                for b in range(d + 1, 8):
                    ratio, ratio_d = held[a, b] * inverse, held[d, b] * inverse_d
                    for c in range(b, 8):
                        held[b, c] = held[b, c] - ratio * held[a, c] - ratio_d * held[d, c]
                    line[b] = line[b] - ratio * line[a] - ratio_d * line[d]
                    columns[b] = [
                        x - ratio * y - ratio_d * z
                        for x, y, z in zip(columns[b], columns[a], columns[d])
                    ]
                scaled += [line[a] * inverse, line[d] * inverse_d]
                final += [line[a] * lax.rsqrt(held[a, a]), line[d] * lax.rsqrt(held[d, d])]
            for h in range(g + 1, end):
                taken = add_up([columns[a][h - g - 1] * scaled[a] for a in range(8)])
                rows[h] = jnp.where(inside, 0.0, rows[h]) - taken
            rows[g] = pile(final)
            if aside:
                aside.pop(0)()
            lefts.append(jnp.where(lane >= 8 * end, rows[g], 0.0))
            rights.append(jnp.where((lane >= k + 8) & (lane < 8 * end), 0.0, rows[g]))
        if end < n_groups:
            taken = dot32(jnp.concatenate(lefts), jnp.concatenate(rights), 0)
            inside = (lane >= 8 * begin) & (lane < 8 * end)
            for h in range(end, n_groups):
                rows[h] = jnp.where(inside, 0.0, rows[h]) - taken[8 * h : 8 * h + 8]
    result = jnp.concatenate(rows, axis=0)
    r = lax.broadcasted_iota(jnp.int32, (BLOCK, BLOCK), 0)
    c = lax.broadcasted_iota(jnp.int32, (BLOCK, BLOCK), 1)
    return jnp.where(c <= r, result, 0.0)


def dot32(a, b, dim=1):
    return lax.dot_general(
        a, b, (((dim,), (0,)), ((), ())), precision=HI, preferred_element_type=jnp.float32
    )


def inverse_kernel(
    n, n_tp, core_ref, own_ref, other_ref, high_out, low_out,
    work, scale, corners, spare, high_ref, low_ref, sems,
):
    per_pair = n_tp // (n // 2)
    strip = BLOCK // per_pair
    half = strip // 2
    core = core_ref[0]
    for t in range(n_tp):
        first, second, offset = place(t, per_pair, n, strip)
        width = (n - first) * BLOCK
        for source, c in ((own_ref, core), (other_ref, 1 - core)):
            for row, lanes in ((first, slice(0, width)), (second, slice(width, None))):
                start = pl.multiple_of(row * BLOCK + offset + c * half, half)
                work[pl.ds(start, half), row * BLOCK :] = source[t, :, lanes]

    r = lax.broadcasted_iota(jnp.int32, (BLOCK, BLOCK), 0)
    c = lax.broadcasted_iota(jnp.int32, (BLOCK, BLOCK), 1)
    tall = []
    for i in range(n):
        rows = slice(i * BLOCK, (i + 1) * BLOCK)
        diagonal = jnp.where(r == c, work[rows, rows], 0.0)
        scale[:, rows] = lax.rsqrt(jnp.sum(diagonal, axis=0, keepdims=True))
        tall.append(lax.rsqrt(jnp.sum(diagonal, axis=1, keepdims=True)))
    for i in range(n):
        rows, rest = slice(i * BLOCK, (i + 1) * BLOCK), slice(i * BLOCK, None)
        work[rows, rest] = work[rows, rest] * tall[i] * scale[:, rest]

    wide = 2 * BLOCK
    n_wide = n // 2
    spans = [slice(i * wide, (i + 1) * wide) for i in range(n_wide)]

    def advance(k, j):
        work[spans[k], spans[j]] = dot32(corners[k % 2], work[spans[k], spans[j]])

    def take(k, i, j):
        change = dot32(work[spans[k], spans[i]], work[spans[k], spans[j]], 0)
        if j == k:
            work[spans[i], spans[j]] = -change
        else:
            work[spans[i], spans[j]] -= change

    def copies(k):
        return [
            pltpu.make_async_copy(part.at[spans[k]], out.at[spans[k]], sems.at[p, k])
            for p, (part, out) in enumerate(((high_ref, high_out), (low_ref, low_out)))
        ]

    def finish(k):
        width = (k + 1) * wide
        high, low = split_parts(work[spans[k], :width] * scale[:, :width])
        high_ref[spans[k], :width] = high
        low_ref[spans[k], :width] = low
        if k + 1 < n_wide:
            rest = jnp.zeros((wide, n * BLOCK - width), jnp.bfloat16)
            high_ref[spans[k], width:] = rest
            low_ref[spans[k], width:] = rest
        for copy in copies(k):
            copy.start()

    aside = []
    for k in range(n_wide):
        here, corner = spans[k], corners.at[k % 2]
        top, bottom = slice(k * wide, k * wide + BLOCK), slice(k * wide + BLOCK, (k + 1) * wide)
        one = invert_factor(work[top, top], spare, aside)
        cross = dot32(one, work[top, bottom])
        two = invert_factor(work[bottom, bottom] - dot32(cross, cross, 0), spare, aside)
        while aside:
            aside.pop(0)()
        corner[:BLOCK, :BLOCK] = one
        corner[:BLOCK, BLOCK:] = jnp.zeros((BLOCK, BLOCK), jnp.float32)
        corner[BLOCK:, BLOCK:] = two
        corner[BLOCK:, :BLOCK] = -dot32(two, dot32(cross, one, 0))
        work[here, here] = corner[...]
        if k + 1 < n_wide:
            advance(k, k + 1)
            take(k, k + 1, k + 1)
        others = [j for j in range(n_wide) if j not in (k, k + 1)]
        aside += [functools.partial(advance, k, j) for j in others]
        aside += [
            functools.partial(take, k, i, j)
            for i in range(k + 1, n_wide)
            for j in range(n_wide)
            if (j <= k or j >= i) and (i, j) != (k + 1, k + 1)
        ]
        aside.append(functools.partial(finish, k))
    while aside:
        aside.pop(0)()
    for k in range(n_wide):
        for copy in copies(k):
            copy.wait()


def inverse_factor(core, own, other, rank):
    n_tp = own.shape[0]
    n = rank // BLOCK
    return pl.pallas_call(
        functools.partial(inverse_kernel, n, n_tp),
        out_shape=[jax.ShapeDtypeStruct((rank, rank), jnp.bfloat16)] * 2,
        in_specs=[pl.BlockSpec(memory_space=pltpu.SMEM)]
        + [pl.BlockSpec(memory_space=pltpu.VMEM)] * 2,
        out_specs=[pl.BlockSpec(memory_space=pl.ANY)] * 2,
        scratch_shapes=[
            pltpu.VMEM((rank, rank), jnp.float32),
            pltpu.VMEM((1, rank), jnp.float32),
            pltpu.VMEM((2, 2 * BLOCK, 2 * BLOCK), jnp.float32),
            pltpu.VMEM((144, BLOCK), jnp.float32),
            pltpu.VMEM((rank, rank), jnp.bfloat16),
            pltpu.VMEM((rank, rank), jnp.bfloat16),
            pltpu.SemaphoreType.DMA((2, n // 2)),
        ],
        compiler_params=pltpu.CompilerParams(vmem_limit_bytes=32 * 1024 * 1024),
        cost_estimate=pl.CostEstimate(
            flops=12 * rank**3, bytes_accessed=8 * rank**2, transcendentals=0
        ),
    )(core, own, other)


def dot16(a, b):
    return lax.dot_general(a, b, (((1,), (1,)), ((), ())), preferred_element_type=jnp.float32)


def right_kernel(chunk, back_ref, high_ref, low_ref, right_ref, squares_ref, back_high, back_low):
    rows = right_ref.shape[0]

    @pl.when(pl.program_id(0) == 0)
    def _():
        for start in range(0, rows, chunk):
            core, z = divmod(start, rows // 2)
            source = (2 * (z // chunk) + core) * chunk
            high, low = split_parts(back_ref[source : source + chunk, :])
            back_high[start : start + chunk, :] = high
            back_low[start : start + chunk, :] = low

    total = dot16(back_high[...], high_ref[...])
    total += dot16(back_high[...], low_ref[...])
    total += dot16(back_low[...], high_ref[...])
    right_ref[...] = total
    squares = jnp.sum(total * total, axis=0, keepdims=True)
    for t in range(squares_ref.shape[0]):
        squares_ref[t] = squares


def project(back, high, low, rows, chunk, n_tp):
    rank = back.shape[1]
    wide = 2 * BLOCK
    whole = pl.BlockSpec(back.shape, lambda j: (0, 0))
    block = pl.BlockSpec((wide, rank), lambda j: (j, 0))
    return pl.pallas_call(
        functools.partial(right_kernel, chunk),
        out_shape=[
            jax.ShapeDtypeStruct((rows, rank), jnp.float32),
            jax.ShapeDtypeStruct((n_tp, 1, rank), jnp.float32),
        ],
        grid=(rank // wide,),
        in_specs=[whole, block, block],
        out_specs=[
            pl.BlockSpec((rows, wide), lambda j: (0, j)),
            pl.BlockSpec((n_tp, 1, wide), lambda j: (0, 0, j)),
        ],
        scratch_shapes=[pltpu.VMEM((rows, rank), jnp.bfloat16)] * 2,
        compiler_params=pltpu.CompilerParams(vmem_limit_bytes=24 * 1024 * 1024),
        cost_estimate=pl.CostEstimate(
            flops=6 * rows * rank**2, bytes_accessed=8 * rank * rows, transcendentals=0
        ),
    )(back, high, low)


def ortho_kernel(left_ref, high_ref, low_ref, ortho_ref):
    total = dot16(left_ref[...], high_ref[...])
    total += dot16(left_ref[...], low_ref[...])
    ortho_ref[...] = total.astype(jnp.bfloat16)


def orthonormal(left, high, low):
    rows, rank = left.shape
    wide = 2 * BLOCK
    block = pl.BlockSpec((wide, rank), lambda j: (j, 0))
    return pl.pallas_call(
        ortho_kernel,
        out_shape=jax.ShapeDtypeStruct((rows, rank), jnp.bfloat16),
        grid=(rank // wide,),
        in_specs=[pl.BlockSpec(left.shape, lambda j: (0, 0)), block, block],
        out_specs=pl.BlockSpec((rows, wide), lambda j: (0, j)),
        compiler_params=pltpu.CompilerParams(vmem_limit_bytes=24 * 1024 * 1024),
        cost_estimate=pl.CostEstimate(flops=0, bytes_accessed=0, transcendentals=0),
    )(left, high, low)


def per_device(momentum, grad, basis):
    n_fsdp, n_tp = lax.axis_size("fsdp"), lax.axis_size("tp")
    n_z = n_fsdp // 2
    z_groups, core_groups = groups(n_fsdp)
    swap = [(i, i ^ 1) for i in range(n_fsdp)]
    rows, cols = momentum.shape
    share = basis.shape[1]
    rank = share * n_fsdp
    rows_all, cols_all = rows * n_fsdp, cols * n_tp
    me_fsdp, me_tp = lax.axis_index("fsdp"), lax.axis_index("tp")
    by_rows = (((0,), (0,)), ((), ()))
    by_cols = (((1,), (1,)), ((), ()))

    def dot(a, b, dims):
        return lax.dot_general(a, b, dims, preferred_element_type=jnp.float32)

    total = momentum.astype(jnp.float32) + grad.astype(jnp.float32)
    total_b = total.astype(jnp.bfloat16)
    basis_all = lax.all_gather(basis, "fsdp", axis=1, tiled=True)
    part = jnp.dot(total_b, basis_all, preferred_element_type=jnp.float32).astype(jnp.bfloat16)
    arrived = exchange(part.reshape(n_tp, rows // n_tp, rank), "tp")
    left_own = jnp.sum(arrived.astype(jnp.float32), axis=0).astype(jnp.bfloat16)
    left = collect(left_own, "tp", n_tp).reshape(rows, rank)

    n = rank // BLOCK
    per_pair = n_tp // (n // 2)
    strip = BLOCK // per_pair
    pair, mirror, offset = place(me_tp, per_pair, n, strip)
    made = []
    for row in (pair, mirror):
        mine = lax.dynamic_slice_in_dim(left, row * BLOCK + offset, strip, 1)
        made.append(dot(mine, left, by_rows))
    packed = lax.select_n(
        pair,
        *[
            jnp.concatenate([made[0][:, p * BLOCK :], made[1][:, (n - 1 - p) * BLOCK :]], axis=1)
            for p in range(n // 2)
        ],
    )
    packed = packed.reshape(2, strip // 2, packed.shape[1])
    packed = jnp.sum(exchange(packed, "fsdp", core_groups), axis=0)
    packed = jnp.sum(collect(packed, "fsdp", n_z, z_groups), axis=0)
    own = collect(packed, "tp", n_tp)
    other = lax.ppermute(own, "fsdp", swap)

    core = me_fsdp % 2
    half = cols // 2
    chunk = -(-half // (32 * n_z)) * 32
    spread = jnp.pad(total_b.reshape(rows, 2, half), ((0, 0), (0, 0), (0, chunk * n_z - half)))
    back = dot(spread.reshape(rows, 2 * chunk * n_z), left, by_rows)
    back = back.reshape(2, chunk * n_z, rank)
    theirs = lax.dynamic_index_in_dim(back, 1 - core, 0, False)
    mine = lax.dynamic_index_in_dim(back, core, 0, False)
    mine = mine + lax.ppermute(theirs, "fsdp", swap)
    mine = lax.psum_scatter(
        mine, "fsdp", scatter_dimension=0, tiled=True, axis_index_groups=z_groups
    )
    back = lax.all_gather(mine, "fsdp", axis=0, tiled=True)

    parity = core.astype(jnp.int32).reshape(1)
    inverse_high, inverse_low = inverse_factor(parity, own, other, rank)
    right, squares = project(back, inverse_high, inverse_low, cols, chunk, n_tp)
    left, squares = lax.optimization_barrier((left, squares))
    squares = exchange(squares, "tp")
    ortho_b = orthonormal(left, inverse_high, inverse_low)
    scale = jnp.sqrt(jnp.sum(squares, axis=(0, 1)) / cols_all + epsilon)
    right_b = right.astype(jnp.bfloat16)
    basis_full = (right / scale[None, :]).astype(jnp.bfloat16)
    basis_new = lax.dynamic_slice_in_dim(basis_full, me_fsdp * share, share, 1)
    correction = dot(ortho_b, right_b, by_cols)
    raw = dot(ortho_b, basis_full, by_cols)
    momentum_new = (total - (1.0 - keep_rate) * correction).astype(jnp.bfloat16)
    update = (math.sqrt(rows_all / rank) * raw).astype(jnp.bfloat16)
    return (momentum_new, basis_new, update)


def solution(mesh):
    return jax.shard_map(
        per_device,
        mesh=mesh,
        in_specs=(P("fsdp", "tp"), P("fsdp", "tp"), P("tp", "fsdp")),
        out_specs=(P("fsdp", "tp"), P("tp", "fsdp"), P("fsdp", "tp")),
        check_vma=False,
    )
```

```python
import functools
import math

import jax
import jax.numpy as jnp
from jax import lax
from jax.experimental import pallas as pl
from jax.experimental.pallas import tpu as pltpu
from jax.sharding import PartitionSpec as P

keep_rate = 0.95
epsilon = 1e-06
BLOCK = 128
VM = 60 * 1024 * 1024
VM1 = 60 * 1024 * 1024
SUB = 8
HI = lax.Precision.HIGHEST


def groups(n_fsdp):
    z_groups = [[2 * z + c for z in range(n_fsdp // 2)] for c in range(2)]
    core_groups = [[2 * z, 2 * z + 1] for z in range(n_fsdp // 2)]
    return z_groups, core_groups


def exchange(pieces, axis, index_groups=None):
    return lax.all_to_all(pieces, axis, 0, 0, tiled=True, axis_index_groups=index_groups)


def collect(own, axis, count, index_groups=None):
    copies = jnp.broadcast_to(own[None], (count,) + own.shape)
    return exchange(copies, axis, index_groups)


def split_parts(value):
    high = value.astype(jnp.bfloat16)
    low = (value - high.astype(jnp.float32)).astype(jnp.bfloat16)
    return high, low


def place(t, per_pair, n, strip):
    pair = t // per_pair
    return pair, n - 1 - pair, (t % per_pair) * strip


def add_up(terms):
    while len(terms) > 1:
        terms = [sum(terms[i + 1 : i + 2], terms[i]) for i in range(0, len(terms), 2)]
    return terms[0]


def invert_factor(block, spare, aside):
    n_groups = BLOCK // 8
    lane = lax.broadcasted_iota(jnp.int32, (8, BLOCK), 1)
    sub = lax.broadcasted_iota(jnp.int32, (8, BLOCK), 0)
    rows = [block[8 * g : 8 * g + 8] for g in range(n_groups)]

    def pile(lines):
        result = lines[0]
        for a in range(1, 8):
            result = jnp.where(sub == a, lines[a], result)
        return result

    for begin in range(0, n_groups, SUB):
        end = begin + SUB
        lefts, rights = [], []
        for g in range(begin, end):
            k = 8 * g
            columns = [
                [jnp.broadcast_to(rows[h][:, k + a : k + a + 1], (8, BLOCK)) for h in range(g, end)]
                for a in range(8)
            ]
            inside = (lane >= k) & (lane < k + 8)
            slot = 72 * (g % 2)
            spare[slot : slot + 8, :] = rows[g]
            for a in range(8):
                spare[slot + 8 + 8 * a : slot + 16 + 8 * a, :] = columns[a][0]

            def spread(row):
                return jnp.broadcast_to(spare[slot + row : slot + row + 1, :], (8, BLOCK))

            line = [
                jnp.where(inside, jnp.where(lane == k + a, 1.0, 0.0), spread(a)) for a in range(8)
            ]
            held = {(a, b): spread(8 + 8 * b + a) for a in range(8) for b in range(a, 8)}
            columns = [column[1:] for column in columns]
            scaled, final = [], []
            for a in range(0, 8, 2):
                d = a + 1
                det = held[a, a] * held[d, d] - held[a, d] * held[a, d]
                inverse = 1.0 / held[a, a]
                inverse_d = held[a, a] * (1.0 / det)
                ratio = held[a, d] * inverse
                for c in range(d, 8):
                    held[d, c] = held[d, c] - ratio * held[a, c]
                line[d] = line[d] - ratio * line[a]
                columns[d] = [x - ratio * y for x, y in zip(columns[d], columns[a])]
                for b in range(d + 1, 8):
                    ratio, ratio_d = held[a, b] * inverse, held[d, b] * inverse_d
                    for c in range(b, 8):
                        held[b, c] = held[b, c] - ratio * held[a, c] - ratio_d * held[d, c]
                    line[b] = line[b] - ratio * line[a] - ratio_d * line[d]
                    columns[b] = [
                        x - ratio * y - ratio_d * z
                        for x, y, z in zip(columns[b], columns[a], columns[d])
                    ]
                scaled += [line[a] * inverse, line[d] * inverse_d]
                final += [line[a] * lax.rsqrt(held[a, a]), line[d] * lax.rsqrt(held[d, d])]
            for h in range(g + 1, end):
                taken = add_up([columns[a][h - g - 1] * scaled[a] for a in range(8)])
                rows[h] = jnp.where(inside, 0.0, rows[h]) - taken
            rows[g] = pile(final)
            if aside:
                aside.pop(0)()
            lefts.append(jnp.where(lane >= 8 * end, rows[g], 0.0))
            rights.append(jnp.where((lane >= k + 8) & (lane < 8 * end), 0.0, rows[g]))
        if end < n_groups:
            taken = dot32(jnp.concatenate(lefts), jnp.concatenate(rights), 0)
            inside = (lane >= 8 * begin) & (lane < 8 * end)
            for h in range(end, n_groups):
                rows[h] = jnp.where(inside, 0.0, rows[h]) - taken[8 * h : 8 * h + 8]
    result = jnp.concatenate(rows, axis=0)
    r = lax.broadcasted_iota(jnp.int32, (BLOCK, BLOCK), 0)
    c = lax.broadcasted_iota(jnp.int32, (BLOCK, BLOCK), 1)
    return jnp.where(c <= r, result, 0.0)


def dot32(a, b, dim=1):
    return lax.dot_general(
        a, b, (((dim,), (0,)), ((), ())), precision=HI, preferred_element_type=jnp.float32
    )


def inverse_kernel(
    n, n_tp, core_ref, own_ref, other_ref, high_out, low_out,
    work, scale, corners, spare, high_ref, low_ref, sems,
):
    per_pair = n_tp // (n // 2)
    strip = BLOCK // per_pair
    half = strip // 2
    core = core_ref[0]
    for t in range(n_tp):
        first, second, offset = place(t, per_pair, n, strip)
        width = (n - first) * BLOCK
        for source, c in ((own_ref, core), (other_ref, 1 - core)):
            for row, lanes in ((first, slice(0, width)), (second, slice(width, None))):
                start = pl.multiple_of(row * BLOCK + offset + c * half, half)
                work[pl.ds(start, half), row * BLOCK :] = source[t, :, lanes]

    r = lax.broadcasted_iota(jnp.int32, (BLOCK, BLOCK), 0)
    c = lax.broadcasted_iota(jnp.int32, (BLOCK, BLOCK), 1)
    tall = []
    for i in range(n):
        rows = slice(i * BLOCK, (i + 1) * BLOCK)
        diagonal = jnp.where(r == c, work[rows, rows], 0.0)
        scale[:, rows] = lax.rsqrt(jnp.sum(diagonal, axis=0, keepdims=True))
        tall.append(lax.rsqrt(jnp.sum(diagonal, axis=1, keepdims=True)))
    for i in range(n):
        rows, rest = slice(i * BLOCK, (i + 1) * BLOCK), slice(i * BLOCK, None)
        work[rows, rest] = work[rows, rest] * tall[i] * scale[:, rest]

    wide = 2 * BLOCK
    n_wide = n // 2
    spans = [slice(i * wide, (i + 1) * wide) for i in range(n_wide)]

    def advance(k, j):
        work[spans[k], spans[j]] = dot32(corners[k % 2], work[spans[k], spans[j]])

    def take(k, i, j):
        change = dot32(work[spans[k], spans[i]], work[spans[k], spans[j]], 0)
        if j == k:
            work[spans[i], spans[j]] = -change
        else:
            work[spans[i], spans[j]] -= change

    def copies(k):
        return [
            pltpu.make_async_copy(part.at[spans[k]], out.at[spans[k]], sems.at[p, k])
            for p, (part, out) in enumerate(((high_ref, high_out), (low_ref, low_out)))
        ]

    def finish(k):
        width = (k + 1) * wide
        high, low = split_parts(work[spans[k], :width] * scale[:, :width])
        high_ref[spans[k], :width] = high
        low_ref[spans[k], :width] = low
        if k + 1 < n_wide:
            rest = jnp.zeros((wide, n * BLOCK - width), jnp.bfloat16)
            high_ref[spans[k], width:] = rest
            low_ref[spans[k], width:] = rest
        for copy in copies(k):
            copy.start()

    aside = []
    for k in range(n_wide):
        here, corner = spans[k], corners.at[k % 2]
        top, bottom = slice(k * wide, k * wide + BLOCK), slice(k * wide + BLOCK, (k + 1) * wide)
        one = invert_factor(work[top, top], spare, aside)
        cross = dot32(one, work[top, bottom])
        two = invert_factor(work[bottom, bottom] - dot32(cross, cross, 0), spare, aside)
        while aside:
            aside.pop(0)()
        corner[:BLOCK, :BLOCK] = one
        corner[:BLOCK, BLOCK:] = jnp.zeros((BLOCK, BLOCK), jnp.float32)
        corner[BLOCK:, BLOCK:] = two
        corner[BLOCK:, :BLOCK] = -dot32(two, dot32(cross, one, 0))
        work[here, here] = corner[...]
        if k + 1 < n_wide:
            advance(k, k + 1)
            take(k, k + 1, k + 1)
        others = [j for j in range(n_wide) if j not in (k, k + 1)]
        aside += [functools.partial(advance, k, j) for j in others]
        aside += [
            functools.partial(take, k, i, j)
            for i in range(k + 1, n_wide)
            for j in range(n_wide)
            if (j <= k or j >= i) and (i, j) != (k + 1, k + 1)
        ]
        aside.append(functools.partial(finish, k))
    while aside:
        aside.pop(0)()
    for k in range(n_wide):
        for copy in copies(k):
            copy.wait()


def inverse_factor(core, own, other, rank):
    n_tp = own.shape[0]
    n = rank // BLOCK
    return pl.pallas_call(
        functools.partial(inverse_kernel, n, n_tp),
        out_shape=[jax.ShapeDtypeStruct((rank, rank), jnp.bfloat16)] * 2,
        in_specs=[pl.BlockSpec(memory_space=pltpu.SMEM)]
        + [pl.BlockSpec(memory_space=pltpu.VMEM)] * 2,
        out_specs=[pl.BlockSpec(memory_space=pltpu.HBM)] * 2,
        scratch_shapes=[
            pltpu.VMEM((rank, rank), jnp.float32),
            pltpu.VMEM((1, rank), jnp.float32),
            pltpu.VMEM((2, 2 * BLOCK, 2 * BLOCK), jnp.float32),
            pltpu.VMEM((144, BLOCK), jnp.float32),
            pltpu.VMEM((rank, rank), jnp.bfloat16),
            pltpu.VMEM((rank, rank), jnp.bfloat16),
            pltpu.SemaphoreType.DMA((2, n // 2)),
        ],
        compiler_params=pltpu.CompilerParams(vmem_limit_bytes=VM1),
        cost_estimate=pl.CostEstimate(
            flops=12 * rank**3, bytes_accessed=8 * rank**2, transcendentals=0
        ),
    )(core, own, other)


def dot16(a, b):
    return lax.dot_general(a, b, (((1,), (1,)), ((), ())), preferred_element_type=jnp.float32)


def right_kernel(chunk, back_ref, high_ref, low_ref, right_ref, squares_ref, back_high, back_low):
    rows = right_ref.shape[0]

    @pl.when(pl.program_id(0) == 0)
    def _():
        for start in range(0, rows, chunk):
            core, z = divmod(start, rows // 2)
            source = (2 * (z // chunk) + core) * chunk
            high, low = split_parts(back_ref[source : source + chunk, :])
            back_high[start : start + chunk, :] = high
            back_low[start : start + chunk, :] = low

    total = dot16(back_high[...], high_ref[...])
    total += dot16(back_high[...], low_ref[...])
    total += dot16(back_low[...], high_ref[...])
    right_ref[...] = total
    squares = jnp.sum(total * total, axis=0, keepdims=True)
    for t in range(squares_ref.shape[0]):
        squares_ref[t] = squares


def project(back, high, low, rows, chunk, n_tp):
    rank = back.shape[1]
    wide = 2 * BLOCK
    whole = pl.BlockSpec(back.shape, lambda j: (0, 0))
    block = pl.BlockSpec((wide, rank), lambda j: (j, 0))
    return pl.pallas_call(
        functools.partial(right_kernel, chunk),
        out_shape=[
            jax.ShapeDtypeStruct((rows, rank), jnp.float32),
            jax.ShapeDtypeStruct((n_tp, 1, rank), jnp.float32),
        ],
        grid=(rank // wide,),
        in_specs=[whole, block, block],
        out_specs=[
            pl.BlockSpec((rows, wide), lambda j: (0, j)),
            pl.BlockSpec((n_tp, 1, wide), lambda j: (0, 0, j)),
        ],
        scratch_shapes=[pltpu.VMEM((rows, rank), jnp.bfloat16)] * 2,
        compiler_params=pltpu.CompilerParams(vmem_limit_bytes=VM),
        cost_estimate=pl.CostEstimate(
            flops=6 * rows * rank**2, bytes_accessed=8 * rank * rows, transcendentals=0
        ),
    )(back, high, low)


def momentum_kernel(
    left_ref, high_ref, low_ref, right_ref, momentum_ref, grad_ref, ortho_ref, out_ref, total
):
    step = pl.program_id(0)
    ortho = dot16(left_ref[...], high_ref[...])
    ortho += dot16(left_ref[...], low_ref[...])
    ortho_b = ortho.astype(jnp.bfloat16)
    ortho_ref[...] = ortho_b
    change = dot16(right_ref[...].astype(jnp.bfloat16), ortho_b)

    @pl.when(step == 0)
    def _():
        total[...] = change

    @pl.when(step > 0)
    def _():
        total[...] += change

    @pl.when(step == pl.num_programs(0) - 1)
    def _():
        kept = momentum_ref[...].astype(jnp.float32) + grad_ref[...].astype(jnp.float32)
        out_ref[...] = (kept - (1.0 - keep_rate) * total[...]).astype(jnp.bfloat16)


def new_momentum(left, high, low, right, momentum, grad):
    rows, rank = left.shape
    cols = right.shape[0]
    wide = 2 * BLOCK
    block = pl.BlockSpec((wide, rank), lambda j: (j, 0))
    whole = pl.BlockSpec((cols, rows), lambda j: (0, 0))
    return pl.pallas_call(
        momentum_kernel,
        out_shape=[
            jax.ShapeDtypeStruct((rows, rank), jnp.bfloat16),
            jax.ShapeDtypeStruct((cols, rows), jnp.bfloat16),
        ],
        grid=(rank // wide,),
        in_specs=[
            pl.BlockSpec((rows, rank), lambda j: (0, 0)),
            block,
            block,
            pl.BlockSpec((cols, wide), lambda j: (0, j)),
            whole,
            whole,
        ],
        out_specs=[pl.BlockSpec((rows, wide), lambda j: (0, j)), whole],
        scratch_shapes=[pltpu.VMEM((cols, rows), jnp.float32)],
        compiler_params=pltpu.CompilerParams(vmem_limit_bytes=VM),
        cost_estimate=pl.CostEstimate(
            flops=4 * rows * rank**2 + 2 * rows * cols * rank,
            bytes_accessed=10 * rank * rows,
            transcendentals=0,
        ),
    )(left, high, low, right, momentum.T, grad.T)


def per_device(momentum, grad, basis):
    n_fsdp, n_tp = lax.axis_size("fsdp"), lax.axis_size("tp")
    n_z = n_fsdp // 2
    z_groups, core_groups = groups(n_fsdp)
    swap = [(i, i ^ 1) for i in range(n_fsdp)]
    rows, cols = momentum.shape
    share = basis.shape[1]
    rank = share * n_fsdp
    rows_all, cols_all = rows * n_fsdp, cols * n_tp
    me_fsdp, me_tp = lax.axis_index("fsdp"), lax.axis_index("tp")
    by_rows = (((0,), (0,)), ((), ()))
    by_cols = (((1,), (1,)), ((), ()))

    def dot(a, b, dims):
        return lax.dot_general(a, b, dims, preferred_element_type=jnp.float32)

    total = momentum.astype(jnp.float32) + grad.astype(jnp.float32)
    total_b = total.astype(jnp.bfloat16)
    basis_all = lax.all_gather(basis, "fsdp", axis=1, tiled=True)
    part = jnp.dot(total_b, basis_all, preferred_element_type=jnp.float32).astype(jnp.bfloat16)
    arrived = exchange(part.reshape(n_tp, rows // n_tp, rank), "tp")
    left_own = jnp.sum(arrived.astype(jnp.float32), axis=0).astype(jnp.bfloat16)
    left = collect(left_own, "tp", n_tp).reshape(rows, rank)

    n = rank // BLOCK
    per_pair = n_tp // (n // 2)
    strip = BLOCK // per_pair
    pair, mirror, offset = place(me_tp, per_pair, n, strip)
    made = []
    for row in (pair, mirror):
        mine = lax.dynamic_slice_in_dim(left, row * BLOCK + offset, strip, 1)
        made.append(dot(mine, left, by_rows))
    packed = lax.select_n(
        pair,
        *[
            jnp.concatenate([made[0][:, p * BLOCK :], made[1][:, (n - 1 - p) * BLOCK :]], axis=1)
            for p in range(n // 2)
        ],
    )
    core = me_fsdp % 2
    half = cols // 2
    chunk = -(-half // (32 * n_z)) * 32
    spread = jnp.pad(total_b.reshape(rows, 2, half), ((0, 0), (0, 0), (0, chunk * n_z - half)))
    back = dot(spread.reshape(rows, 2 * chunk * n_z), left, by_rows)
    back = back.reshape(2, chunk * n_z, rank)
    theirs = lax.dynamic_index_in_dim(back, 1 - core, 0, False)
    mine = lax.dynamic_index_in_dim(back, core, 0, False)
    theirs = lax.ppermute(theirs, "fsdp", swap)
    packed = packed.reshape(2, strip // 2, packed.shape[1])
    packed = jnp.sum(exchange(packed, "fsdp", core_groups), axis=0)
    packed, theirs = lax.optimization_barrier((packed, theirs))
    mine = mine + theirs
    mine = lax.psum_scatter(
        mine, "fsdp", scatter_dimension=0, tiled=True, axis_index_groups=z_groups
    )
    back = lax.all_gather(mine, "fsdp", axis=0, tiled=True)

    packed = jnp.sum(collect(packed, "fsdp", n_z, z_groups), axis=0)
    own = collect(packed, "tp", n_tp)
    other = lax.ppermute(own, "fsdp", swap)

    parity = core.astype(jnp.int32).reshape(1)
    inverse_high, inverse_low = inverse_factor(parity, own, other, rank)
    right, squares = project(back, inverse_high, inverse_low, cols, chunk, n_tp)
    squares = exchange(squares, "tp")
    ortho_b, kept = new_momentum(left, inverse_high, inverse_low, right, momentum, grad)
    scale = jnp.sqrt(jnp.sum(squares, axis=(0, 1)) / cols_all + epsilon)
    basis_full = (right / scale[None, :]).astype(jnp.bfloat16)
    basis_new = lax.dynamic_slice_in_dim(basis_full, me_fsdp * share, share, 1)
    raw = dot(ortho_b, basis_full, by_cols)
    update = (math.sqrt(rows_all / rank) * raw).astype(jnp.bfloat16)
    return (kept.T, basis_new, update)


def solution(mesh):
    return jax.shard_map(
        per_device,
        mesh=mesh,
        in_specs=(P("fsdp", "tp"), P("fsdp", "tp"), P("tp", "fsdp")),
        out_specs=(P("fsdp", "tp"), P("tp", "fsdp"), P("fsdp", "tp")),
        check_vma=False,
    )
```

```python
import functools
import math

import jax
import jax.numpy as jnp
from jax import lax
from jax.experimental import pallas as pl
from jax.experimental.pallas import tpu as pltpu
from jax.sharding import PartitionSpec as P

keep_rate = 0.95
epsilon = 1e-06
BLOCK = 128
VM = 60 * 1024 * 1024
VM1 = 51 * 1024 * 1024
SUB = 8
HI = lax.Precision.HIGH


def groups(n_fsdp):
    z_groups = [[2 * z + c for z in range(n_fsdp // 2)] for c in range(2)]
    core_groups = [[2 * z, 2 * z + 1] for z in range(n_fsdp // 2)]
    return z_groups, core_groups


def exchange(pieces, axis, index_groups=None):
    return lax.all_to_all(pieces, axis, 0, 0, tiled=True, axis_index_groups=index_groups)


def collect(own, axis, count, index_groups=None):
    copies = jnp.broadcast_to(own[None], (count,) + own.shape)
    return exchange(copies, axis, index_groups)


def split_parts(value):
    high = value.astype(jnp.bfloat16)
    low = (value - high.astype(jnp.float32)).astype(jnp.bfloat16)
    return high, low


def place(t, per_pair, n, strip):
    pair = t // per_pair
    return pair, n - 1 - pair, (t % per_pair) * strip


def add_up(terms):
    while len(terms) > 1:
        terms = [sum(terms[i + 1 : i + 2], terms[i]) for i in range(0, len(terms), 2)]
    return terms[0]


def invert_factor(block, spare, aside):
    n_groups = BLOCK // 8
    lane = lax.broadcasted_iota(jnp.int32, (8, BLOCK), 1)
    sub = lax.broadcasted_iota(jnp.int32, (8, BLOCK), 0)
    rows = [block[8 * g : 8 * g + 8] for g in range(n_groups)]

    def pile(lines):
        result = lines[0]
        for a in range(1, 8):
            result = jnp.where(sub == a, lines[a], result)
        return result

    for begin in range(0, n_groups, SUB):
        end = begin + SUB
        lefts, rights = [], []
        for g in range(begin, end):
            k = 8 * g
            columns = [
                [jnp.broadcast_to(rows[h][:, k + a : k + a + 1], (8, BLOCK)) for h in range(g, end)]
                for a in range(8)
            ]
            inside = (lane >= k) & (lane < k + 8)
            slot = 72 * (g % 2)
            spare[slot : slot + 8, :] = rows[g]
            for a in range(8):
                spare[slot + 8 + 8 * a : slot + 16 + 8 * a, :] = columns[a][0]

            def spread(row):
                return jnp.broadcast_to(spare[slot + row : slot + row + 1, :], (8, BLOCK))

            line = [
                jnp.where(inside, jnp.where(lane == k + a, 1.0, 0.0), spread(a)) for a in range(8)
            ]
            held = {(a, b): spread(8 + 8 * b + a) for a in range(8) for b in range(a, 8)}
            columns = [column[1:] for column in columns]
            scaled, final = [], []
            for a in range(0, 8, 2):
                d = a + 1
                det = held[a, a] * held[d, d] - held[a, d] * held[a, d]
                inverse = 1.0 / held[a, a]
                inverse_d = held[a, a] * (1.0 / det)
                ratio = held[a, d] * inverse
                for c in range(d, 8):
                    held[d, c] = held[d, c] - ratio * held[a, c]
                line[d] = line[d] - ratio * line[a]
                columns[d] = [x - ratio * y for x, y in zip(columns[d], columns[a])]
                for b in range(d + 1, 8):
                    ratio, ratio_d = held[a, b] * inverse, held[d, b] * inverse_d
                    for c in range(b, 8):
                        held[b, c] = held[b, c] - ratio * held[a, c] - ratio_d * held[d, c]
                    line[b] = line[b] - ratio * line[a] - ratio_d * line[d]
                    columns[b] = [
                        x - ratio * y - ratio_d * z
                        for x, y, z in zip(columns[b], columns[a], columns[d])
                    ]
                scaled += [line[a] * inverse, line[d] * inverse_d]
                final += [line[a] * lax.rsqrt(held[a, a]), line[d] * lax.rsqrt(held[d, d])]
            for h in range(g + 1, end):
                taken = add_up([columns[a][h - g - 1] * scaled[a] for a in range(8)])
                rows[h] = jnp.where(inside, 0.0, rows[h]) - taken
            rows[g] = pile(final)
            if aside:
                aside.pop(0)()
            lefts.append(jnp.where(lane >= 8 * end, rows[g], 0.0))
            rights.append(jnp.where((lane >= k + 8) & (lane < 8 * end), 0.0, rows[g]))
        if end < n_groups:
            taken = dot32(jnp.concatenate(lefts), jnp.concatenate(rights), 0)
            inside = (lane >= 8 * begin) & (lane < 8 * end)
            for h in range(end, n_groups):
                rows[h] = jnp.where(inside, 0.0, rows[h]) - taken[8 * h : 8 * h + 8]
    result = jnp.concatenate(rows, axis=0)
    r = lax.broadcasted_iota(jnp.int32, (BLOCK, BLOCK), 0)
    c = lax.broadcasted_iota(jnp.int32, (BLOCK, BLOCK), 1)
    return jnp.where(c <= r, result, 0.0)


def dot32(a, b, dim=1):
    return lax.dot_general(
        a, b, (((dim,), (0,)), ((), ())), precision=HI, preferred_element_type=jnp.float32
    )


def inverse_kernel(
    n, n_tp, core_ref, own_ref, other_ref, high_out, low_out,
    work, scale, corners, spare, high_ref, low_ref, sems,
):
    per_pair = n_tp // (n // 2)
    strip = BLOCK // per_pair
    half = strip // 2
    core = core_ref[0]
    for t in range(n_tp):
        first, second, offset = place(t, per_pair, n, strip)
        width = (n - first) * BLOCK
        for source, c in ((own_ref, core), (other_ref, 1 - core)):
            for row, lanes in ((first, slice(0, width)), (second, slice(width, None))):
                start = pl.multiple_of(row * BLOCK + offset + c * half, half)
                work[pl.ds(start, half), row * BLOCK :] = source[t, :, lanes]

    r = lax.broadcasted_iota(jnp.int32, (BLOCK, BLOCK), 0)
    c = lax.broadcasted_iota(jnp.int32, (BLOCK, BLOCK), 1)
    tall = []
    for i in range(n):
        rows = slice(i * BLOCK, (i + 1) * BLOCK)
        diagonal = jnp.where(r == c, work[rows, rows], 0.0)
        scale[:, rows] = lax.rsqrt(jnp.sum(diagonal, axis=0, keepdims=True))
        tall.append(lax.rsqrt(jnp.sum(diagonal, axis=1, keepdims=True)))
    for i in range(n):
        rows, rest = slice(i * BLOCK, (i + 1) * BLOCK), slice(i * BLOCK, None)
        work[rows, rest] = work[rows, rest] * tall[i] * scale[:, rest]

    wide = 2 * BLOCK
    n_wide = n // 2
    spans = [slice(i * wide, (i + 1) * wide) for i in range(n_wide)]

    def advance(k, j):
        work[spans[k], spans[j]] = dot32(corners[k % 2], work[spans[k], spans[j]])

    def take(k, i, j):
        change = dot32(work[spans[k], spans[i]], work[spans[k], spans[j]], 0)
        if j == k:
            work[spans[i], spans[j]] = -change
        else:
            work[spans[i], spans[j]] -= change

    def copies(k):
        return [
            pltpu.make_async_copy(part.at[spans[k]], out.at[spans[k]], sems.at[p, k])
            for p, (part, out) in enumerate(((high_ref, high_out), (low_ref, low_out)))
        ]

    def finish(k):
        width = (k + 1) * wide
        high, low = split_parts(work[spans[k], :width] * scale[:, :width])
        high_ref[spans[k], :width] = high
        low_ref[spans[k], :width] = low
        if k + 1 < n_wide:
            rest = jnp.zeros((wide, n * BLOCK - width), jnp.bfloat16)
            high_ref[spans[k], width:] = rest
            low_ref[spans[k], width:] = rest
        for copy in copies(k):
            copy.start()

    aside = []
    for k in range(n_wide):
        here, corner = spans[k], corners.at[k % 2]
        top, bottom = slice(k * wide, k * wide + BLOCK), slice(k * wide + BLOCK, (k + 1) * wide)
        one = invert_factor(work[top, top], spare, aside)
        cross = dot32(one, work[top, bottom])
        two = invert_factor(work[bottom, bottom] - dot32(cross, cross, 0), spare, aside)
        while aside:
            aside.pop(0)()
        corner[:BLOCK, :BLOCK] = one
        corner[:BLOCK, BLOCK:] = jnp.zeros((BLOCK, BLOCK), jnp.float32)
        corner[BLOCK:, BLOCK:] = two
        corner[BLOCK:, :BLOCK] = -dot32(two, dot32(cross, one, 0))
        work[here, here] = corner[...]
        if k + 1 < n_wide:
            advance(k, k + 1)
            take(k, k + 1, k + 1)
        others = [j for j in range(n_wide) if j not in (k, k + 1)]
        aside += [functools.partial(advance, k, j) for j in others]
        aside += [
            functools.partial(take, k, i, j)
            for i in range(k + 1, n_wide)
            for j in range(n_wide)
            if (j <= k or j >= i) and (i, j) != (k + 1, k + 1)
        ]
        aside.append(functools.partial(finish, k))
    while aside:
        aside.pop(0)()
    for k in range(n_wide):
        for copy in copies(k):
            copy.wait()


def inverse_factor(core, own, other, rank):
    n_tp = own.shape[0]
    n = rank // BLOCK
    return pl.pallas_call(
        functools.partial(inverse_kernel, n, n_tp),
        out_shape=[jax.ShapeDtypeStruct((rank, rank), jnp.bfloat16)] * 2,
        in_specs=[pl.BlockSpec(memory_space=pltpu.SMEM)]
        + [pl.BlockSpec(memory_space=pltpu.VMEM)] * 2,
        out_specs=[pl.BlockSpec(memory_space=pltpu.HBM)] * 2,
        scratch_shapes=[
            pltpu.VMEM((rank, rank), jnp.float32),
            pltpu.VMEM((1, rank), jnp.float32),
            pltpu.VMEM((2, 2 * BLOCK, 2 * BLOCK), jnp.float32),
            pltpu.VMEM((144, BLOCK), jnp.float32),
            pltpu.VMEM((rank, rank), jnp.bfloat16),
            pltpu.VMEM((rank, rank), jnp.bfloat16),
            pltpu.SemaphoreType.DMA((2, n // 2)),
        ],
        compiler_params=pltpu.CompilerParams(vmem_limit_bytes=VM1),
        cost_estimate=pl.CostEstimate(
            flops=12 * rank**3, bytes_accessed=8 * rank**2, transcendentals=0
        ),
    )(core, own, other)


def dot16(a, b):
    return lax.dot_general(a, b, (((1,), (1,)), ((), ())), preferred_element_type=jnp.float32)


def right_kernel(chunk, back_ref, high_ref, low_ref, right_ref, squares_ref, back_high, back_low):
    rows = right_ref.shape[0]

    @pl.when(pl.program_id(0) == 0)
    def _():
        for start in range(0, rows, chunk):
            core, z = divmod(start, rows // 2)
            source = (2 * (z // chunk) + core) * chunk
            high, low = split_parts(back_ref[source : source + chunk, :])
            back_high[start : start + chunk, :] = high
            back_low[start : start + chunk, :] = low

    total = dot16(back_high[...], high_ref[...])
    total += dot16(back_high[...], low_ref[...])
    total += dot16(back_low[...], high_ref[...])
    right_ref[...] = total
    squares = jnp.sum(total * total, axis=0, keepdims=True)
    for t in range(squares_ref.shape[0]):
        squares_ref[t] = squares


def project(back, high, low, rows, chunk, n_tp):
    rank = back.shape[1]
    wide = 2 * BLOCK
    whole = pl.BlockSpec(back.shape, lambda j: (0, 0))
    block = pl.BlockSpec((wide, rank), lambda j: (j, 0))
    return pl.pallas_call(
        functools.partial(right_kernel, chunk),
        out_shape=[
            jax.ShapeDtypeStruct((rows, rank), jnp.float32),
            jax.ShapeDtypeStruct((n_tp, 1, rank), jnp.float32),
        ],
        grid=(rank // wide,),
        in_specs=[whole, block, block],
        out_specs=[
            pl.BlockSpec((rows, wide), lambda j: (0, j)),
            pl.BlockSpec((n_tp, 1, wide), lambda j: (0, 0, j)),
        ],
        scratch_shapes=[pltpu.VMEM((rows, rank), jnp.bfloat16)] * 2,
        compiler_params=pltpu.CompilerParams(vmem_limit_bytes=VM),
        cost_estimate=pl.CostEstimate(
            flops=6 * rows * rank**2, bytes_accessed=8 * rank * rows, transcendentals=0
        ),
    )(back, high, low)


def momentum_kernel(
    left_ref, high_ref, low_ref, right_ref, momentum_ref, grad_ref, ortho_ref, out_ref, total
):
    step = pl.program_id(0)
    ortho = dot16(left_ref[...], high_ref[...])
    ortho += dot16(left_ref[...], low_ref[...])
    ortho_b = ortho.astype(jnp.bfloat16)
    ortho_ref[...] = ortho_b
    change = dot16(right_ref[...].astype(jnp.bfloat16), ortho_b)

    @pl.when(step == 0)
    def _():
        total[...] = change

    @pl.when(step > 0)
    def _():
        total[...] += change

    @pl.when(step == pl.num_programs(0) - 1)
    def _():
        kept = momentum_ref[...].astype(jnp.float32) + grad_ref[...].astype(jnp.float32)
        out_ref[...] = (kept - (1.0 - keep_rate) * total[...]).astype(jnp.bfloat16)


def new_momentum(left, high, low, right, momentum, grad):
    rows, rank = left.shape
    cols = right.shape[0]
    wide = 2 * BLOCK
    block = pl.BlockSpec((wide, rank), lambda j: (j, 0))
    whole = pl.BlockSpec((cols, rows), lambda j: (0, 0))
    return pl.pallas_call(
        momentum_kernel,
        out_shape=[
            jax.ShapeDtypeStruct((rows, rank), jnp.bfloat16),
            jax.ShapeDtypeStruct((cols, rows), jnp.bfloat16),
        ],
        grid=(rank // wide,),
        in_specs=[
            pl.BlockSpec((rows, rank), lambda j: (0, 0)),
            block,
            block,
            pl.BlockSpec((cols, wide), lambda j: (0, j)),
            whole,
            whole,
        ],
        out_specs=[pl.BlockSpec((rows, wide), lambda j: (0, j)), whole],
        scratch_shapes=[pltpu.VMEM((cols, rows), jnp.float32)],
        compiler_params=pltpu.CompilerParams(vmem_limit_bytes=VM),
        cost_estimate=pl.CostEstimate(
            flops=4 * rows * rank**2 + 2 * rows * cols * rank,
            bytes_accessed=10 * rank * rows,
            transcendentals=0,
        ),
    )(left, high, low, right, momentum.T, grad.T)


def by_rows(a, b):
    return lax.dot_general(a, b, (((0,), (0,)), ((), ())), preferred_element_type=jnp.float32)


def left_kernel(n, place_ref, left_ref, spread_ref, packed_ref, mine_ref, theirs_ref, strips):
    pair, offset, core = place_ref[0], place_ref[1], place_ref[2]
    half = packed_ref.shape[1]
    for s, row in enumerate((pair, n - 1 - pair)):
        lanes = pl.ds(pl.multiple_of(row * BLOCK, BLOCK), BLOCK)
        strips[s] = by_rows(left_ref[:, lanes], left_ref[...])
    for p in range(n // 2):

        @pl.when(pair == p)
        def _():
            width = (n - p) * BLOCK
            for h in range(2):
                rows = pl.ds(pl.multiple_of(offset + h * half, half), half)
                packed_ref[h, :, :width] = strips[0, rows, p * BLOCK :]
                packed_ref[h, :, width:] = strips[1, rows, (n - 1 - p) * BLOCK :]

    wide = mine_ref.shape[0]
    for target, part in ((theirs_ref, 1 - core), (mine_ref, core)):
        lanes = pl.ds(pl.multiple_of(part * wide, wide), wide)
        target[...] = by_rows(spread_ref[:, lanes], left_ref[...])


def from_left(where, left, spread, n, strip):
    rank = left.shape[1]
    wide = spread.shape[1] // 2
    half = jax.ShapeDtypeStruct((wide, rank), jnp.float32)
    return pl.pallas_call(
        functools.partial(left_kernel, n),
        out_shape=[
            jax.ShapeDtypeStruct((2, strip // 2, (n + 1) * BLOCK), jnp.float32),
            half,
            half,
        ],
        in_specs=[pl.BlockSpec(memory_space=pltpu.SMEM)]
        + [pl.BlockSpec(memory_space=pltpu.VMEM)] * 2,
        out_specs=[pl.BlockSpec(memory_space=pltpu.VMEM)] * 3,
        scratch_shapes=[pltpu.VMEM((2, BLOCK, rank), jnp.float32)],
        compiler_params=pltpu.CompilerParams(vmem_limit_bytes=16 * 1024 * 1024),
        cost_estimate=pl.CostEstimate(
            flops=2 * left.shape[0] * rank * (2 * BLOCK + 2 * wide),
            bytes_accessed=8 * rank * left.shape[0],
            transcendentals=0,
        ),
    )(where, left, spread)


def per_device(momentum, grad, basis):
    n_fsdp, n_tp = lax.axis_size("fsdp"), lax.axis_size("tp")
    n_z = n_fsdp // 2
    z_groups, core_groups = groups(n_fsdp)
    swap = [(i, i ^ 1) for i in range(n_fsdp)]
    rows, cols = momentum.shape
    share = basis.shape[1]
    rank = share * n_fsdp
    rows_all, cols_all = rows * n_fsdp, cols * n_tp
    me_fsdp, me_tp = lax.axis_index("fsdp"), lax.axis_index("tp")
    by_cols = (((1,), (1,)), ((), ()))

    def dot(a, b, dims):
        return lax.dot_general(a, b, dims, preferred_element_type=jnp.float32)

    total = momentum.astype(jnp.float32) + grad.astype(jnp.float32)
    total_b = total.astype(jnp.bfloat16)
    basis_all = lax.all_gather(basis, "fsdp", axis=1, tiled=True)
    part = jnp.dot(total_b, basis_all, preferred_element_type=jnp.float32).astype(jnp.bfloat16)
    arrived = exchange(part.reshape(n_tp, rows // n_tp, rank), "tp")
    left_own = jnp.sum(arrived.astype(jnp.float32), axis=0).astype(jnp.bfloat16)
    left = collect(left_own, "tp", n_tp).reshape(rows, rank)

    n = rank // BLOCK
    per_pair = n_tp // (n // 2)
    strip = BLOCK // per_pair
    pair, _, offset = place(me_tp, per_pair, n, strip)
    core = me_fsdp % 2
    half = cols // 2
    chunk = -(-half // (32 * n_z)) * 32
    spread = jnp.pad(total_b.reshape(rows, 2, half), ((0, 0), (0, 0), (0, chunk * n_z - half)))
    where = jnp.stack([pair, offset, core]).astype(jnp.int32)
    packed, mine, theirs = from_left(where, left, spread.reshape(rows, 2 * chunk * n_z), n, strip)
    theirs = lax.ppermute(theirs, "fsdp", swap)
    packed = jnp.sum(exchange(packed, "fsdp", core_groups), axis=0)
    packed, theirs = lax.optimization_barrier((packed, theirs))
    mine = mine + theirs
    mine = lax.psum_scatter(
        mine, "fsdp", scatter_dimension=0, tiled=True, axis_index_groups=z_groups
    )
    back = lax.all_gather(mine, "fsdp", axis=0, tiled=True)

    packed = jnp.sum(collect(packed, "fsdp", n_z, z_groups), axis=0)
    own = collect(packed, "tp", n_tp)
    other = lax.ppermute(own, "fsdp", swap)

    parity = core.astype(jnp.int32).reshape(1)
    inverse_high, inverse_low = inverse_factor(parity, own, other, rank)
    right, squares = project(back, inverse_high, inverse_low, cols, chunk, n_tp)
    squares = exchange(squares, "tp")
    ortho_b, kept = new_momentum(left, inverse_high, inverse_low, right, momentum, grad)
    scale = jnp.sqrt(jnp.sum(squares, axis=(0, 1)) / cols_all + epsilon)
    basis_full = (right / scale[None, :]).astype(jnp.bfloat16)
    basis_new = lax.dynamic_slice_in_dim(basis_full, me_fsdp * share, share, 1)
    raw = dot(ortho_b, basis_full, by_cols)
    update = (math.sqrt(rows_all / rank) * raw).astype(jnp.bfloat16)
    return (kept.T, basis_new, update)


def solution(mesh):
    return jax.shard_map(
        per_device,
        mesh=mesh,
        in_specs=(P("fsdp", "tp"), P("fsdp", "tp"), P("tp", "fsdp")),
        out_specs=(P("fsdp", "tp"), P("tp", "fsdp"), P("fsdp", "tp")),
        check_vma=False,
    )
```

```python
import functools
import math

import jax
import jax.numpy as jnp
from jax import lax
from jax.experimental import pallas as pl
from jax.experimental.pallas import tpu as pltpu
from jax.sharding import PartitionSpec as P

keep_rate = 0.95
epsilon = 1e-06
BLOCK = 128
VM = 60 * 1024 * 1024
VM1 = 51 * 1024 * 1024
SUB = 8
HI = lax.Precision.HIGH


def groups(n_fsdp):
    z_groups = [[2 * z + c for z in range(n_fsdp // 2)] for c in range(2)]
    core_groups = [[2 * z, 2 * z + 1] for z in range(n_fsdp // 2)]
    return z_groups, core_groups


def exchange(pieces, axis, index_groups=None):
    return lax.all_to_all(pieces, axis, 0, 0, tiled=True, axis_index_groups=index_groups)


def collect(own, axis, count, index_groups=None):
    copies = jnp.broadcast_to(own[None], (count,) + own.shape)
    return exchange(copies, axis, index_groups)


def split_parts(value):
    high = value.astype(jnp.bfloat16)
    low = (value - high.astype(jnp.float32)).astype(jnp.bfloat16)
    return high, low


def place(t, per_pair, n, strip):
    pair = t // per_pair
    return pair, n - 1 - pair, (t % per_pair) * strip


def add_up(terms):
    while len(terms) > 1:
        terms = [sum(terms[i + 1 : i + 2], terms[i]) for i in range(0, len(terms), 2)]
    return terms[0]


def invert_factor(block, spare, aside):
    n_groups = BLOCK // 8
    lane = lax.broadcasted_iota(jnp.int32, (8, BLOCK), 1)
    sub = lax.broadcasted_iota(jnp.int32, (8, BLOCK), 0)
    rows = [block[8 * g : 8 * g + 8] for g in range(n_groups)]

    def pile(lines):
        result = lines[0]
        for a in range(1, 8):
            result = jnp.where(sub == a, lines[a], result)
        return result

    for begin in range(0, n_groups, SUB):
        end = begin + SUB
        lefts, rights = [], []
        for g in range(begin, end):
            k = 8 * g
            columns = [
                [jnp.broadcast_to(rows[h][:, k + a : k + a + 1], (8, BLOCK)) for h in range(g, end)]
                for a in range(8)
            ]
            inside = (lane >= k) & (lane < k + 8)
            slot = 72 * (g % 2)
            spare[slot : slot + 8, :] = rows[g]
            for a in range(8):
                spare[slot + 8 + 8 * a : slot + 16 + 8 * a, :] = columns[a][0]

            def spread(row):
                return jnp.broadcast_to(spare[slot + row : slot + row + 1, :], (8, BLOCK))

            line = [
                jnp.where(inside, jnp.where(lane == k + a, 1.0, 0.0), spread(a)) for a in range(8)
            ]
            held = {(a, b): spread(8 + 8 * b + a) for a in range(8) for b in range(a, 8)}
            columns = [column[1:] for column in columns]
            scaled, final = [], []
            for a in range(0, 8, 2):
                d = a + 1
                det = held[a, a] * held[d, d] - held[a, d] * held[a, d]
                inverse = 1.0 / held[a, a]
                inverse_d = held[a, a] * (1.0 / det)
                ratio = held[a, d] * inverse
                for c in range(d, 8):
                    held[d, c] = held[d, c] - ratio * held[a, c]
                line[d] = line[d] - ratio * line[a]
                columns[d] = [x - ratio * y for x, y in zip(columns[d], columns[a])]
                for b in range(d + 1, 8):
                    ratio, ratio_d = held[a, b] * inverse, held[d, b] * inverse_d
                    for c in range(b, 8):
                        held[b, c] = held[b, c] - ratio * held[a, c] - ratio_d * held[d, c]
                    line[b] = line[b] - ratio * line[a] - ratio_d * line[d]
                    columns[b] = [
                        x - ratio * y - ratio_d * z
                        for x, y, z in zip(columns[b], columns[a], columns[d])
                    ]
                scaled += [line[a] * inverse, line[d] * inverse_d]
                final += [line[a] * lax.rsqrt(held[a, a]), line[d] * lax.rsqrt(held[d, d])]
            for h in range(g + 1, end):
                taken = add_up([columns[a][h - g - 1] * scaled[a] for a in range(8)])
                rows[h] = jnp.where(inside, 0.0, rows[h]) - taken
            rows[g] = pile(final)
            if aside:
                aside.pop(0)()
            lefts.append(jnp.where(lane >= 8 * end, rows[g], 0.0))
            rights.append(jnp.where((lane >= k + 8) & (lane < 8 * end), 0.0, rows[g]))
        if end < n_groups:
            taken = dot32(jnp.concatenate(lefts), jnp.concatenate(rights), 0)
            inside = (lane >= 8 * begin) & (lane < 8 * end)
            for h in range(end, n_groups):
                rows[h] = jnp.where(inside, 0.0, rows[h]) - taken[8 * h : 8 * h + 8]
    result = jnp.concatenate(rows, axis=0)
    r = lax.broadcasted_iota(jnp.int32, (BLOCK, BLOCK), 0)
    c = lax.broadcasted_iota(jnp.int32, (BLOCK, BLOCK), 1)
    return jnp.where(c <= r, result, 0.0)


def dot32(a, b, dim=1):
    return lax.dot_general(
        a, b, (((dim,), (0,)), ((), ())), precision=HI, preferred_element_type=jnp.float32
    )


def inverse_kernel(
    n, n_tp, core_ref, own_ref, other_ref, high_out, low_out,
    work, scale, corners, spare, high_ref, low_ref, sems,
):
    per_pair = n_tp // (n // 2)
    strip = BLOCK // per_pair
    half = strip // 2
    core = core_ref[0]

    def load(row):
        for t in range(n_tp):
            first, second, offset = place(t, per_pair, n, strip)
            if row not in (first, second):
                continue
            width = (n - first) * BLOCK
            lanes = slice(0, width) if row == first else slice(width, None)
            for source, c in ((own_ref, core), (other_ref, 1 - core)):
                start = pl.multiple_of(row * BLOCK + offset + c * half, half)
                work[pl.ds(start, half), row * BLOCK :] = source[t, :, lanes]

    r = lax.broadcasted_iota(jnp.int32, (BLOCK, BLOCK), 0)
    c = lax.broadcasted_iota(jnp.int32, (BLOCK, BLOCK), 1)
    tall = {}

    def measure(row):
        rows = slice(row * BLOCK, (row + 1) * BLOCK)
        diagonal = jnp.where(r == c, work[rows, rows], 0.0)
        scale[:, rows] = lax.rsqrt(jnp.sum(diagonal, axis=0, keepdims=True))
        tall[row] = lax.rsqrt(jnp.sum(diagonal, axis=1, keepdims=True))

    def normalise(row, lanes):
        rows = slice(row * BLOCK, (row + 1) * BLOCK)
        work[rows, lanes] = work[rows, lanes] * tall[row] * scale[:, lanes]

    wide = 2 * BLOCK
    n_wide = n // 2
    spans = [slice(i * wide, (i + 1) * wide) for i in range(n_wide)]

    def advance(k, j):
        work[spans[k], spans[j]] = dot32(corners[k % 2], work[spans[k], spans[j]])

    def take(k, i, j):
        change = dot32(work[spans[k], spans[i]], work[spans[k], spans[j]], 0)
        if j == k:
            work[spans[i], spans[j]] = -change
        else:
            work[spans[i], spans[j]] -= change

    def copies(k):
        return [
            pltpu.make_async_copy(part.at[spans[k]], out.at[spans[k]], sems.at[p, k])
            for p, (part, out) in enumerate(((high_ref, high_out), (low_ref, low_out)))
        ]

    def finish(k):
        width = (k + 1) * wide
        high, low = split_parts(work[spans[k], :width] * scale[:, :width])
        high_ref[spans[k], :width] = high
        low_ref[spans[k], :width] = low
        if k + 1 < n_wide:
            rest = jnp.zeros((wide, n * BLOCK - width), jnp.bfloat16)
            high_ref[spans[k], width:] = rest
            low_ref[spans[k], width:] = rest
        for copy in copies(k):
            copy.start()

    for row in range(2):
        load(row)
        measure(row)
    for row in range(2):
        normalise(row, slice(row * BLOCK, wide))
    aside = [functools.partial(load, row) for row in range(2, n)]
    aside += [functools.partial(measure, row) for row in range(2, n)]
    aside += [
        functools.partial(normalise, row, slice(max(row, 2) * BLOCK, None)) for row in range(n)
    ]
    for k in range(n_wide):
        here, corner = spans[k], corners.at[k % 2]
        top, bottom = slice(k * wide, k * wide + BLOCK), slice(k * wide + BLOCK, (k + 1) * wide)
        one = invert_factor(work[top, top], spare, aside)
        cross = dot32(one, work[top, bottom])
        two = invert_factor(work[bottom, bottom] - dot32(cross, cross, 0), spare, aside)
        while aside:
            aside.pop(0)()
        corner[:BLOCK, :BLOCK] = one
        corner[:BLOCK, BLOCK:] = jnp.zeros((BLOCK, BLOCK), jnp.float32)
        corner[BLOCK:, BLOCK:] = two
        corner[BLOCK:, :BLOCK] = -dot32(two, dot32(cross, one, 0))
        work[here, here] = corner[...]
        if k + 1 < n_wide:
            advance(k, k + 1)
            take(k, k + 1, k + 1)
        others = [j for j in range(n_wide) if j not in (k, k + 1)]
        aside += [functools.partial(advance, k, j) for j in others]
        aside += [
            functools.partial(take, k, i, j)
            for i in range(k + 1, n_wide)
            for j in range(n_wide)
            if (j <= k or j >= i) and (i, j) != (k + 1, k + 1)
        ]
        aside.append(functools.partial(finish, k))
    while aside:
        aside.pop(0)()
    for k in range(n_wide):
        for copy in copies(k):
            copy.wait()


def inverse_factor(core, own, other, rank):
    n_tp = own.shape[0]
    n = rank // BLOCK
    return pl.pallas_call(
        functools.partial(inverse_kernel, n, n_tp),
        out_shape=[jax.ShapeDtypeStruct((rank, rank), jnp.bfloat16)] * 2,
        in_specs=[pl.BlockSpec(memory_space=pltpu.SMEM)]
        + [pl.BlockSpec(memory_space=pltpu.VMEM)] * 2,
        out_specs=[pl.BlockSpec(memory_space=pltpu.HBM)] * 2,
        scratch_shapes=[
            pltpu.VMEM((rank, rank), jnp.float32),
            pltpu.VMEM((1, rank), jnp.float32),
            pltpu.VMEM((2, 2 * BLOCK, 2 * BLOCK), jnp.float32),
            pltpu.VMEM((144, BLOCK), jnp.float32),
            pltpu.VMEM((rank, rank), jnp.bfloat16),
            pltpu.VMEM((rank, rank), jnp.bfloat16),
            pltpu.SemaphoreType.DMA((2, n // 2)),
        ],
        compiler_params=pltpu.CompilerParams(vmem_limit_bytes=VM1),
        cost_estimate=pl.CostEstimate(
            flops=12 * rank**3, bytes_accessed=8 * rank**2, transcendentals=0
        ),
    )(core, own, other)


def dot16(a, b):
    return lax.dot_general(a, b, (((1,), (1,)), ((), ())), preferred_element_type=jnp.float32)


def right_kernel(chunk, back_ref, high_ref, low_ref, right_ref, squares_ref, back_high, back_low):
    rows = right_ref.shape[0]

    @pl.when(pl.program_id(0) == 0)
    def _():
        for start in range(0, rows, chunk):
            core, z = divmod(start, rows // 2)
            source = (2 * (z // chunk) + core) * chunk
            high, low = split_parts(back_ref[source : source + chunk, :])
            back_high[start : start + chunk, :] = high
            back_low[start : start + chunk, :] = low

    wide, rank = high_ref.shape
    for j in range(rank // wide):

        @pl.when(pl.program_id(0) == j)
        def _():
            depth = slice(0, (j + 1) * wide)
            total = dot16(back_high[:, depth], high_ref[:, depth])
            total += dot16(back_high[:, depth], low_ref[:, depth])
            total += dot16(back_low[:, depth], high_ref[:, depth])
            right_ref[...] = total
            squares = jnp.sum(total * total, axis=0, keepdims=True)
            for t in range(squares_ref.shape[0]):
                squares_ref[t] = squares


def project(back, high, low, rows, chunk, n_tp):
    rank = back.shape[1]
    wide = 4 * BLOCK
    whole = pl.BlockSpec(back.shape, lambda j: (0, 0))
    block = pl.BlockSpec((wide, rank), lambda j: (j, 0))
    return pl.pallas_call(
        functools.partial(right_kernel, chunk),
        out_shape=[
            jax.ShapeDtypeStruct((rows, rank), jnp.float32),
            jax.ShapeDtypeStruct((n_tp, 1, rank), jnp.float32),
        ],
        grid=(rank // wide,),
        in_specs=[whole, block, block],
        out_specs=[
            pl.BlockSpec((rows, wide), lambda j: (0, j)),
            pl.BlockSpec((n_tp, 1, wide), lambda j: (0, 0, j)),
        ],
        scratch_shapes=[pltpu.VMEM((rows, rank), jnp.bfloat16)] * 2,
        compiler_params=pltpu.CompilerParams(vmem_limit_bytes=VM),
        cost_estimate=pl.CostEstimate(
            flops=6 * rows * rank**2, bytes_accessed=8 * rank * rows, transcendentals=0
        ),
    )(back, high, low)


def momentum_kernel(
    left_ref, high_ref, low_ref, right_ref, momentum_ref, grad_ref, ortho_ref, out_ref, total
):
    wide, rank = high_ref.shape
    steps = rank // wide
    for j in range(steps):

        @pl.when(pl.program_id(0) == j)
        def _():
            depth = slice(0, (j + 1) * wide)
            ortho = dot16(left_ref[:, depth], high_ref[:, depth])
            ortho += dot16(left_ref[:, depth], low_ref[:, depth])
            ortho_b = ortho.astype(jnp.bfloat16)
            ortho_ref[...] = ortho_b
            change = dot16(right_ref[...].astype(jnp.bfloat16), ortho_b)
            if j > 0:
                change += total[...]
            if j + 1 < steps:
                total[...] = change
            else:
                kept = momentum_ref[...].astype(jnp.float32) + grad_ref[...].astype(jnp.float32)
                out_ref[...] = (kept - (1.0 - keep_rate) * change).astype(jnp.bfloat16)


def new_momentum(left, high, low, right, momentum, grad):
    rows, rank = left.shape
    cols = right.shape[0]
    wide = 4 * BLOCK
    block = pl.BlockSpec((wide, rank), lambda j: (j, 0))
    whole = pl.BlockSpec((cols, rows), lambda j: (0, 0))
    return pl.pallas_call(
        momentum_kernel,
        out_shape=[
            jax.ShapeDtypeStruct((rows, rank), jnp.bfloat16),
            jax.ShapeDtypeStruct((cols, rows), jnp.bfloat16),
        ],
        grid=(rank // wide,),
        in_specs=[
            pl.BlockSpec((rows, rank), lambda j: (0, 0)),
            block,
            block,
            pl.BlockSpec((cols, wide), lambda j: (0, j)),
            whole,
            whole,
        ],
        out_specs=[pl.BlockSpec((rows, wide), lambda j: (0, j)), whole],
        scratch_shapes=[pltpu.VMEM((cols, rows), jnp.float32)],
        compiler_params=pltpu.CompilerParams(vmem_limit_bytes=VM),
        cost_estimate=pl.CostEstimate(
            flops=4 * rows * rank**2 + 2 * rows * cols * rank,
            bytes_accessed=10 * rank * rows,
            transcendentals=0,
        ),
    )(left, high, low, right, momentum.T, grad.T)


def by_rows(a, b):
    return lax.dot_general(a, b, (((0,), (0,)), ((), ())), preferred_element_type=jnp.float32)


def left_kernel(n, place_ref, left_ref, spread_ref, packed_ref, mine_ref, theirs_ref, strips):
    pair, offset, core = place_ref[0], place_ref[1], place_ref[2]
    half = packed_ref.shape[1]
    for s, row in enumerate((pair, n - 1 - pair)):
        lanes = pl.ds(pl.multiple_of(row * BLOCK, BLOCK), BLOCK)
        strips[s] = by_rows(left_ref[:, lanes], left_ref[...])
    for p in range(n // 2):

        @pl.when(pair == p)
        def _():
            width = (n - p) * BLOCK
            for h in range(2):
                rows = pl.ds(pl.multiple_of(offset + h * half, half), half)
                packed_ref[h, :, :width] = strips[0, rows, p * BLOCK :]
                packed_ref[h, :, width:] = strips[1, rows, (n - 1 - p) * BLOCK :]

    wide = mine_ref.shape[0]
    for target, part in ((theirs_ref, 1 - core), (mine_ref, core)):
        lanes = pl.ds(pl.multiple_of(part * wide, wide), wide)
        target[...] = by_rows(spread_ref[:, lanes], left_ref[...])


def from_left(where, left, spread, n, strip):
    rank = left.shape[1]
    wide = spread.shape[1] // 2
    half = jax.ShapeDtypeStruct((wide, rank), jnp.float32)
    return pl.pallas_call(
        functools.partial(left_kernel, n),
        out_shape=[
            jax.ShapeDtypeStruct((2, strip // 2, (n + 1) * BLOCK), jnp.float32),
            half,
            half,
        ],
        in_specs=[pl.BlockSpec(memory_space=pltpu.SMEM)]
        + [pl.BlockSpec(memory_space=pltpu.VMEM)] * 2,
        out_specs=[pl.BlockSpec(memory_space=pltpu.VMEM)] * 3,
        scratch_shapes=[pltpu.VMEM((2, BLOCK, rank), jnp.float32)],
        compiler_params=pltpu.CompilerParams(vmem_limit_bytes=16 * 1024 * 1024),
        cost_estimate=pl.CostEstimate(
            flops=2 * left.shape[0] * rank * (2 * BLOCK + 2 * wide),
            bytes_accessed=8 * rank * left.shape[0],
            transcendentals=0,
        ),
    )(where, left, spread)


def per_device(momentum, grad, basis):
    n_fsdp, n_tp = lax.axis_size("fsdp"), lax.axis_size("tp")
    n_z = n_fsdp // 2
    z_groups, core_groups = groups(n_fsdp)
    swap = [(i, i ^ 1) for i in range(n_fsdp)]
    rows, cols = momentum.shape
    share = basis.shape[1]
    rank = share * n_fsdp
    rows_all, cols_all = rows * n_fsdp, cols * n_tp
    me_fsdp, me_tp = lax.axis_index("fsdp"), lax.axis_index("tp")
    by_cols = (((1,), (1,)), ((), ()))

    def dot(a, b, dims):
        return lax.dot_general(a, b, dims, preferred_element_type=jnp.float32)

    total = momentum.astype(jnp.float32) + grad.astype(jnp.float32)
    total_b = total.astype(jnp.bfloat16)
    basis_all = lax.all_gather(basis, "fsdp", axis=1, tiled=True)
    part = jnp.dot(total_b, basis_all, preferred_element_type=jnp.float32).astype(jnp.bfloat16)
    arrived = exchange(part.reshape(n_tp, rows // n_tp, rank), "tp")
    left_own = jnp.sum(arrived.astype(jnp.float32), axis=0).astype(jnp.bfloat16)
    left = collect(left_own, "tp", n_tp).reshape(rows, rank)

    n = rank // BLOCK
    per_pair = n_tp // (n // 2)
    strip = BLOCK // per_pair
    pair, _, offset = place(me_tp, per_pair, n, strip)
    core = me_fsdp % 2
    half = cols // 2
    chunk = -(-half // (32 * n_z)) * 32
    spread = jnp.pad(total_b.reshape(rows, 2, half), ((0, 0), (0, 0), (0, chunk * n_z - half)))
    where = jnp.stack([pair, offset, core]).astype(jnp.int32)
    packed, mine, theirs = from_left(where, left, spread.reshape(rows, 2 * chunk * n_z), n, strip)
    theirs = lax.ppermute(theirs, "fsdp", swap)
    packed = jnp.sum(exchange(packed, "fsdp", core_groups), axis=0)
    packed, theirs = lax.optimization_barrier((packed, theirs))
    mine = mine + theirs
    mine = lax.psum_scatter(
        mine, "fsdp", scatter_dimension=0, tiled=True, axis_index_groups=z_groups
    )
    back = lax.all_gather(mine, "fsdp", axis=0, tiled=True)

    packed = jnp.sum(collect(packed, "fsdp", n_z, z_groups), axis=0)
    own = collect(packed, "tp", n_tp)
    other = lax.ppermute(own, "fsdp", swap)

    parity = core.astype(jnp.int32).reshape(1)
    inverse_high, inverse_low = inverse_factor(parity, own, other, rank)
    right, squares = project(back, inverse_high, inverse_low, cols, chunk, n_tp)
    squares = exchange(squares, "tp")
    ortho_b, kept = new_momentum(left, inverse_high, inverse_low, right, momentum, grad)
    scale = jnp.sqrt(jnp.sum(squares, axis=(0, 1)) / cols_all + epsilon)
    basis_full = (right / scale[None, :]).astype(jnp.bfloat16)
    basis_new = lax.dynamic_slice_in_dim(basis_full, me_fsdp * share, share, 1)
    raw = dot(ortho_b, basis_full, by_cols)
    update = (math.sqrt(rows_all / rank) * raw).astype(jnp.bfloat16)
    return (kept.T, basis_new, update)


def solution(mesh):
    return jax.shard_map(
        per_device,
        mesh=mesh,
        in_specs=(P("fsdp", "tp"), P("fsdp", "tp"), P("tp", "fsdp")),
        out_specs=(P("fsdp", "tp"), P("tp", "fsdp"), P("fsdp", "tp")),
        check_vma=False,
    )
```

```python
import functools
import math

import jax
import jax.numpy as jnp
from jax import lax
from jax.experimental import pallas as pl
from jax.experimental.pallas import tpu as pltpu
from jax.sharding import PartitionSpec as P

keep_rate = 0.95
epsilon = 1e-06
BLOCK = 128
VM = 60 * 1024 * 1024
VM1 = 51 * 1024 * 1024
SUB = 8
HI = lax.Precision.HIGH


def groups(n_fsdp):
    z_groups = [[2 * z + c for z in range(n_fsdp // 2)] for c in range(2)]
    core_groups = [[2 * z, 2 * z + 1] for z in range(n_fsdp // 2)]
    return z_groups, core_groups


def exchange(pieces, axis, index_groups=None):
    return lax.all_to_all(pieces, axis, 0, 0, tiled=True, axis_index_groups=index_groups)


def collect(own, axis, count, index_groups=None):
    copies = jnp.broadcast_to(own[None], (count,) + own.shape)
    return exchange(copies, axis, index_groups)


def split_parts(value):
    high = value.astype(jnp.bfloat16)
    low = (value - high.astype(jnp.float32)).astype(jnp.bfloat16)
    return high, low


def place(t, per_pair, n, strip):
    pair = t // per_pair
    return pair, n - 1 - pair, (t % per_pair) * strip


def add_up(terms):
    while len(terms) > 1:
        terms = [sum(terms[i + 1 : i + 2], terms[i]) for i in range(0, len(terms), 2)]
    return terms[0]


def invert_factor(block, spare, aside):
    n_groups = BLOCK // 8
    lane = lax.broadcasted_iota(jnp.int32, (8, BLOCK), 1)
    sub = lax.broadcasted_iota(jnp.int32, (8, BLOCK), 0)
    rows = [block[8 * g : 8 * g + 8] for g in range(n_groups)]

    def pile(lines):
        result = lines[0]
        for a in range(1, 8):
            result = jnp.where(sub == a, lines[a], result)
        return result

    for begin in range(0, n_groups, SUB):
        end = begin + SUB
        lefts, rights = [], []
        for g in range(begin, end):
            k = 8 * g
            columns = [
                [jnp.broadcast_to(rows[h][:, k + a : k + a + 1], (8, BLOCK)) for h in range(g, end)]
                for a in range(8)
            ]
            inside = (lane >= k) & (lane < k + 8)
            slot = 72 * (g % 2)
            spare[slot : slot + 8, :] = rows[g]
            for a in range(8):
                spare[slot + 8 + 8 * a : slot + 16 + 8 * a, :] = columns[a][0]

            def spread(row):
                return jnp.broadcast_to(spare[slot + row : slot + row + 1, :], (8, BLOCK))

            line = [
                jnp.where(inside, jnp.where(lane == k + a, 1.0, 0.0), spread(a)) for a in range(8)
            ]
            held = {(a, b): spread(8 + 8 * b + a) for a in range(8) for b in range(a, 8)}
            columns = [column[1:] for column in columns]
            scaled, final = [], []
            for a in range(0, 8, 2):
                d = a + 1
                det = held[a, a] * held[d, d] - held[a, d] * held[a, d]
                inverse = 1.0 / held[a, a]
                inverse_d = held[a, a] * (1.0 / det)
                ratio = held[a, d] * inverse
                for c in range(d, 8):
                    held[d, c] = held[d, c] - ratio * held[a, c]
                line[d] = line[d] - ratio * line[a]
                columns[d] = [x - ratio * y for x, y in zip(columns[d], columns[a])]
                for b in range(d + 1, 8):
                    ratio, ratio_d = held[a, b] * inverse, held[d, b] * inverse_d
                    for c in range(b, 8):
                        held[b, c] = held[b, c] - ratio * held[a, c] - ratio_d * held[d, c]
                    line[b] = line[b] - ratio * line[a] - ratio_d * line[d]
                    columns[b] = [
                        x - ratio * y - ratio_d * z
                        for x, y, z in zip(columns[b], columns[a], columns[d])
                    ]
                scaled += [line[a] * inverse, line[d] * inverse_d]
                final += [line[a] * lax.rsqrt(held[a, a]), line[d] * lax.rsqrt(held[d, d])]
            for h in range(g + 1, end):
                taken = add_up([columns[a][h - g - 1] * scaled[a] for a in range(8)])
                rows[h] = jnp.where(inside, 0.0, rows[h]) - taken
            rows[g] = pile(final)
            if aside:
                aside.pop(0)()
            lefts.append(jnp.where(lane >= 8 * end, rows[g], 0.0))
            rights.append(jnp.where((lane >= k + 8) & (lane < 8 * end), 0.0, rows[g]))
        if end < n_groups:
            taken = dot32(jnp.concatenate(lefts), jnp.concatenate(rights), 0)
            inside = (lane >= 8 * begin) & (lane < 8 * end)
            for h in range(end, n_groups):
                rows[h] = jnp.where(inside, 0.0, rows[h]) - taken[8 * h : 8 * h + 8]
    result = jnp.concatenate(rows, axis=0)
    r = lax.broadcasted_iota(jnp.int32, (BLOCK, BLOCK), 0)
    c = lax.broadcasted_iota(jnp.int32, (BLOCK, BLOCK), 1)
    return jnp.where(c <= r, result, 0.0)


def dot32(a, b, dim=1):
    return lax.dot_general(
        a, b, (((dim,), (0,)), ((), ())), precision=HI, preferred_element_type=jnp.float32
    )


def inverse_kernel(
    n, n_tp, core_ref, own_ref, other_ref, high_out, low_out,
    work, scale, corners, spare, high_ref, low_ref, sems,
):
    per_pair = n_tp // (n // 2)
    strip = BLOCK // per_pair
    half = strip // 2
    core = core_ref[0]

    def load(row):
        for t in range(n_tp):
            first, second, offset = place(t, per_pair, n, strip)
            if row not in (first, second):
                continue
            width = (n - first) * BLOCK
            lanes = slice(0, width) if row == first else slice(width, None)
            for source, c in ((own_ref, core), (other_ref, 1 - core)):
                start = pl.multiple_of(row * BLOCK + offset + c * half, half)
                work[pl.ds(start, half), row * BLOCK :] = source[t, :, lanes]

    r = lax.broadcasted_iota(jnp.int32, (BLOCK, BLOCK), 0)
    c = lax.broadcasted_iota(jnp.int32, (BLOCK, BLOCK), 1)
    tall = {}

    def measure(row):
        rows = slice(row * BLOCK, (row + 1) * BLOCK)
        diagonal = jnp.where(r == c, work[rows, rows], 0.0)
        scale[:, rows] = lax.rsqrt(jnp.sum(diagonal, axis=0, keepdims=True))
        tall[row] = lax.rsqrt(jnp.sum(diagonal, axis=1, keepdims=True))

    def normalise(row, lanes):
        rows = slice(row * BLOCK, (row + 1) * BLOCK)
        work[rows, lanes] = work[rows, lanes] * tall[row] * scale[:, lanes]

    wide = 2 * BLOCK
    n_wide = n // 2
    spans = [slice(i * wide, (i + 1) * wide) for i in range(n_wide)]

    def advance(k, j):
        work[spans[k], spans[j]] = dot32(corners[k % 2], work[spans[k], spans[j]])

    def take(k, i, j):
        change = dot32(work[spans[k], spans[i]], work[spans[k], spans[j]], 0)
        if j == k:
            work[spans[i], spans[j]] = -change
        else:
            work[spans[i], spans[j]] -= change

    def copies(k):
        return [
            pltpu.make_async_copy(part.at[spans[k]], out.at[spans[k]], sems.at[p, k])
            for p, (part, out) in enumerate(((high_ref, high_out), (low_ref, low_out)))
        ]

    def pieces(j):
        k = n_wide - 1
        return [
            pltpu.make_async_copy(
                part.at[spans[k], spans[j]], out.at[spans[k], spans[j]], sems.at[p, k + j]
            )
            for p, (part, out) in enumerate(((high_ref, high_out), (low_ref, low_out)))
        ]

    def conclude(j):
        k = n_wide - 1
        if j < k:
            advance(k, j)
        high, low = split_parts(work[spans[k], spans[j]] * scale[:, spans[j]])
        high_ref[spans[k], spans[j]] = high
        low_ref[spans[k], spans[j]] = low
        for copy in pieces(j):
            copy.start()

    def finish(k):
        width = (k + 1) * wide
        high, low = split_parts(work[spans[k], :width] * scale[:, :width])
        high_ref[spans[k], :width] = high
        low_ref[spans[k], :width] = low
        if k + 1 < n_wide:
            rest = jnp.zeros((wide, n * BLOCK - width), jnp.bfloat16)
            high_ref[spans[k], width:] = rest
            low_ref[spans[k], width:] = rest
        for copy in copies(k):
            copy.start()

    for row in range(2):
        load(row)
        measure(row)
    for row in range(2):
        normalise(row, slice(row * BLOCK, wide))
    aside = [functools.partial(load, row) for row in range(2, n)]
    aside += [functools.partial(measure, row) for row in range(2, n)]
    aside += [
        functools.partial(normalise, row, slice(max(row, 2) * BLOCK, None)) for row in range(n)
    ]
    for k in range(n_wide):
        here, corner = spans[k], corners.at[k % 2]
        top, bottom = slice(k * wide, k * wide + BLOCK), slice(k * wide + BLOCK, (k + 1) * wide)
        one = invert_factor(work[top, top], spare, aside)
        cross = dot32(one, work[top, bottom])
        two = invert_factor(work[bottom, bottom] - dot32(cross, cross, 0), spare, aside)
        while aside:
            aside.pop(0)()
        corner[:BLOCK, :BLOCK] = one
        corner[:BLOCK, BLOCK:] = jnp.zeros((BLOCK, BLOCK), jnp.float32)
        corner[BLOCK:, BLOCK:] = two
        corner[BLOCK:, :BLOCK] = -dot32(two, dot32(cross, one, 0))
        work[here, here] = corner[...]
        if k + 1 < n_wide:
            advance(k, k + 1)
            take(k, k + 1, k + 1)
        else:
            aside += [functools.partial(conclude, j) for j in reversed(range(n_wide))]
            continue
        others = [j for j in range(n_wide) if j not in (k, k + 1)]
        aside += [functools.partial(advance, k, j) for j in others]
        aside += [
            functools.partial(take, k, i, j)
            for i in range(k + 1, n_wide)
            for j in range(n_wide)
            if (j <= k or j >= i) and (i, j) != (k + 1, k + 1)
        ]
        aside.append(functools.partial(finish, k))
    while aside:
        aside.pop(0)()
    for k in range(n_wide - 1):
        for copy in copies(k):
            copy.wait()
    for j in range(n_wide):
        for copy in pieces(j):
            copy.wait()


def inverse_factor(core, own, other, rank):
    n_tp = own.shape[0]
    n = rank // BLOCK
    return pl.pallas_call(
        functools.partial(inverse_kernel, n, n_tp),
        out_shape=[jax.ShapeDtypeStruct((rank, rank), jnp.bfloat16)] * 2,
        in_specs=[pl.BlockSpec(memory_space=pltpu.SMEM)]
        + [pl.BlockSpec(memory_space=pltpu.VMEM)] * 2,
        out_specs=[pl.BlockSpec(memory_space=pltpu.HBM)] * 2,
        scratch_shapes=[
            pltpu.VMEM((rank, rank), jnp.float32),
            pltpu.VMEM((1, rank), jnp.float32),
            pltpu.VMEM((2, 2 * BLOCK, 2 * BLOCK), jnp.float32),
            pltpu.VMEM((144, BLOCK), jnp.float32),
            pltpu.VMEM((rank, rank), jnp.bfloat16),
            pltpu.VMEM((rank, rank), jnp.bfloat16),
            pltpu.SemaphoreType.DMA((2, n - 1)),
        ],
        compiler_params=pltpu.CompilerParams(vmem_limit_bytes=VM1),
        cost_estimate=pl.CostEstimate(
            flops=12 * rank**3, bytes_accessed=8 * rank**2, transcendentals=0
        ),
    )(core, own, other)


def dot16(a, b):
    return lax.dot_general(a, b, (((1,), (1,)), ((), ())), preferred_element_type=jnp.float32)


def right_kernel(chunk, back_ref, high_ref, low_ref, right_ref, squares_ref, back_high, back_low):
    rows = right_ref.shape[0]

    @pl.when(pl.program_id(0) == 0)
    def _():
        for start in range(0, rows, chunk):
            core, z = divmod(start, rows // 2)
            source = (2 * (z // chunk) + core) * chunk
            high, low = split_parts(back_ref[source : source + chunk, :])
            back_high[start : start + chunk, :] = high
            back_low[start : start + chunk, :] = low

    wide, rank = high_ref.shape
    for j in range(rank // wide):

        @pl.when(pl.program_id(0) == j)
        def _():
            depth = slice(0, (j + 1) * wide)
            total = dot16(back_high[:, depth], high_ref[:, depth])
            total += dot16(back_high[:, depth], low_ref[:, depth])
            total += dot16(back_low[:, depth], high_ref[:, depth])
            right_ref[...] = total
            squares = jnp.sum(total * total, axis=0, keepdims=True)
            for t in range(squares_ref.shape[0]):
                squares_ref[t] = squares


def project(back, high, low, rows, chunk, n_tp):
    rank = back.shape[1]
    wide = 4 * BLOCK
    whole = pl.BlockSpec(back.shape, lambda j: (0, 0))
    block = pl.BlockSpec((wide, rank), lambda j: (j, 0))
    return pl.pallas_call(
        functools.partial(right_kernel, chunk),
        out_shape=[
            jax.ShapeDtypeStruct((rows, rank), jnp.float32),
            jax.ShapeDtypeStruct((n_tp, 1, rank), jnp.float32),
        ],
        grid=(rank // wide,),
        in_specs=[whole, block, block],
        out_specs=[
            pl.BlockSpec((rows, wide), lambda j: (0, j)),
            pl.BlockSpec((n_tp, 1, wide), lambda j: (0, 0, j)),
        ],
        scratch_shapes=[pltpu.VMEM((rows, rank), jnp.bfloat16)] * 2,
        compiler_params=pltpu.CompilerParams(vmem_limit_bytes=VM),
        cost_estimate=pl.CostEstimate(
            flops=6 * rows * rank**2, bytes_accessed=8 * rank * rows, transcendentals=0
        ),
    )(back, high, low)


def momentum_kernel(
    left_ref, high_ref, low_ref, right_ref, momentum_ref, grad_ref, ortho_ref, out_ref, total
):
    wide, rank = high_ref.shape
    steps = rank // wide
    for j in range(steps):

        @pl.when(pl.program_id(0) == j)
        def _():
            depth = slice(0, (j + 1) * wide)
            ortho = dot16(left_ref[:, depth], high_ref[:, depth])
            ortho += dot16(left_ref[:, depth], low_ref[:, depth])
            ortho_b = ortho.astype(jnp.bfloat16)
            ortho_ref[...] = ortho_b
            change = dot16(right_ref[...].astype(jnp.bfloat16), ortho_b)
            if j > 0:
                change += total[...]
            if j + 1 < steps:
                total[...] = change
            else:
                kept = momentum_ref[...].astype(jnp.float32) + grad_ref[...].astype(jnp.float32)
                out_ref[...] = (kept - (1.0 - keep_rate) * change).astype(jnp.bfloat16)


def new_momentum(left, high, low, right, momentum, grad):
    rows, rank = left.shape
    cols = right.shape[0]
    wide = 4 * BLOCK
    block = pl.BlockSpec((wide, rank), lambda j: (j, 0))
    whole = pl.BlockSpec((cols, rows), lambda j: (0, 0))
    return pl.pallas_call(
        momentum_kernel,
        out_shape=[
            jax.ShapeDtypeStruct((rows, rank), jnp.bfloat16),
            jax.ShapeDtypeStruct((cols, rows), jnp.bfloat16),
        ],
        grid=(rank // wide,),
        in_specs=[
            pl.BlockSpec((rows, rank), lambda j: (0, 0)),
            block,
            block,
            pl.BlockSpec((cols, wide), lambda j: (0, j)),
            whole,
            whole,
        ],
        out_specs=[pl.BlockSpec((rows, wide), lambda j: (0, j)), whole],
        scratch_shapes=[pltpu.VMEM((cols, rows), jnp.float32)],
        compiler_params=pltpu.CompilerParams(vmem_limit_bytes=VM),
        cost_estimate=pl.CostEstimate(
            flops=4 * rows * rank**2 + 2 * rows * cols * rank,
            bytes_accessed=10 * rank * rows,
            transcendentals=0,
        ),
    )(left, high, low, right, momentum.T, grad.T)


def by_rows(a, b):
    return lax.dot_general(a, b, (((0,), (0,)), ((), ())), preferred_element_type=jnp.float32)


def left_kernel(n, place_ref, left_ref, spread_ref, packed_ref, mine_ref, theirs_ref, strips):
    pair, offset, core = place_ref[0], place_ref[1], place_ref[2]
    half = packed_ref.shape[1]
    for s, row in enumerate((pair, n - 1 - pair)):
        lanes = pl.ds(pl.multiple_of(row * BLOCK, BLOCK), BLOCK)
        strips[s] = by_rows(left_ref[:, lanes], left_ref[...])
    for p in range(n // 2):

        @pl.when(pair == p)
        def _():
            width = (n - p) * BLOCK
            for h in range(2):
                rows = pl.ds(pl.multiple_of(offset + h * half, half), half)
                packed_ref[h, :, :width] = strips[0, rows, p * BLOCK :]
                packed_ref[h, :, width:] = strips[1, rows, (n - 1 - p) * BLOCK :]

    wide = mine_ref.shape[0]
    for target, part in ((theirs_ref, 1 - core), (mine_ref, core)):
        lanes = pl.ds(pl.multiple_of(part * wide, wide), wide)
        target[...] = by_rows(spread_ref[:, lanes], left_ref[...])


def from_left(where, left, spread, n, strip):
    rank = left.shape[1]
    wide = spread.shape[1] // 2
    half = jax.ShapeDtypeStruct((wide, rank), jnp.float32)
    return pl.pallas_call(
        functools.partial(left_kernel, n),
        out_shape=[
            jax.ShapeDtypeStruct((2, strip // 2, (n + 1) * BLOCK), jnp.float32),
            half,
            half,
        ],
        in_specs=[pl.BlockSpec(memory_space=pltpu.SMEM)]
        + [pl.BlockSpec(memory_space=pltpu.VMEM)] * 2,
        out_specs=[pl.BlockSpec(memory_space=pltpu.VMEM)] * 3,
        scratch_shapes=[pltpu.VMEM((2, BLOCK, rank), jnp.float32)],
        compiler_params=pltpu.CompilerParams(vmem_limit_bytes=16 * 1024 * 1024),
        cost_estimate=pl.CostEstimate(
            flops=2 * left.shape[0] * rank * (2 * BLOCK + 2 * wide),
            bytes_accessed=8 * rank * left.shape[0],
            transcendentals=0,
        ),
    )(where, left, spread)


def per_device(momentum, grad, basis):
    n_fsdp, n_tp = lax.axis_size("fsdp"), lax.axis_size("tp")
    n_z = n_fsdp // 2
    z_groups, core_groups = groups(n_fsdp)
    swap = [(i, i ^ 1) for i in range(n_fsdp)]
    rows, cols = momentum.shape
    share = basis.shape[1]
    rank = share * n_fsdp
    rows_all, cols_all = rows * n_fsdp, cols * n_tp
    me_fsdp, me_tp = lax.axis_index("fsdp"), lax.axis_index("tp")
    by_cols = (((1,), (1,)), ((), ()))

    def dot(a, b, dims):
        return lax.dot_general(a, b, dims, preferred_element_type=jnp.float32)

    total = momentum.astype(jnp.float32) + grad.astype(jnp.float32)
    total_b = total.astype(jnp.bfloat16)
    basis_all = lax.all_gather(basis, "fsdp", axis=1, tiled=True)
    part = jnp.dot(total_b, basis_all, preferred_element_type=jnp.float32).astype(jnp.bfloat16)
    arrived = exchange(part.reshape(n_tp, rows // n_tp, rank), "tp")
    left_own = jnp.sum(arrived.astype(jnp.float32), axis=0).astype(jnp.bfloat16)
    left = collect(left_own, "tp", n_tp).reshape(rows, rank)

    n = rank // BLOCK
    per_pair = n_tp // (n // 2)
    strip = BLOCK // per_pair
    pair, _, offset = place(me_tp, per_pair, n, strip)
    core = me_fsdp % 2
    half = cols // 2
    chunk = -(-half // (32 * n_z)) * 32
    spread = jnp.pad(total_b.reshape(rows, 2, half), ((0, 0), (0, 0), (0, chunk * n_z - half)))
    where = jnp.stack([pair, offset, core]).astype(jnp.int32)
    packed, mine, theirs = from_left(where, left, spread.reshape(rows, 2 * chunk * n_z), n, strip)
    theirs = lax.ppermute(theirs, "fsdp", swap)
    packed = jnp.sum(exchange(packed, "fsdp", core_groups), axis=0)
    packed, theirs = lax.optimization_barrier((packed, theirs))
    mine = mine + theirs
    mine = lax.psum_scatter(
        mine, "fsdp", scatter_dimension=0, tiled=True, axis_index_groups=z_groups
    )
    back = lax.all_gather(mine, "fsdp", axis=0, tiled=True)

    packed = jnp.sum(collect(packed, "fsdp", n_z, z_groups), axis=0)
    own = collect(packed, "tp", n_tp)
    other = lax.ppermute(own, "fsdp", swap)

    parity = core.astype(jnp.int32).reshape(1)
    inverse_high, inverse_low = inverse_factor(parity, own, other, rank)
    right, squares = project(back, inverse_high, inverse_low, cols, chunk, n_tp)
    squares = exchange(squares, "tp")
    own_columns = lax.dynamic_slice_in_dim(right, me_fsdp * share, share, 1).T
    own_columns = lax.optimization_barrier(own_columns)
    ortho_b, kept = new_momentum(left, inverse_high, inverse_low, right, momentum, grad)
    scale = jnp.sqrt(jnp.sum(squares, axis=(0, 1)) / cols_all + epsilon)
    basis_full = (right / scale[None, :]).astype(jnp.bfloat16)
    basis_new = (own_columns / lax.dynamic_slice_in_dim(scale, me_fsdp * share, share)[:, None]).T
    basis_new = basis_new.astype(jnp.bfloat16)
    raw = dot(ortho_b, basis_full, by_cols)
    update = (math.sqrt(rows_all / rank) * raw).astype(jnp.bfloat16)
    return (kept.T, basis_new, update)


def solution(mesh):
    return jax.shard_map(
        per_device,
        mesh=mesh,
        in_specs=(P("fsdp", "tp"), P("fsdp", "tp"), P("tp", "fsdp")),
        out_specs=(P("fsdp", "tp"), P("tp", "fsdp"), P("fsdp", "tp")),
        check_vma=False,
    )
```
